128 devices in a mesh: gy: 4 (over z), gz: 32 (over x, y, core).
Axes of the slice: x: 4, y: 4, z: 4, core: 2. Of those that a mesh axis runs over, the one named last changes fastest.
Arguments:
- fields: float32 [2, 2, 1024, 2048], P(None, None, 'gz', 'gy'), may hold values from -8 to 8
- cond_x: float32 [2, 2], replicated, may hold values from 0.05 to 0.4
- cond_y: float32 [2, 2, 1024, 2048], P(None, None, 'gz', 'gy'), may hold values from 4096 to 32768
- cond_z: float32 [2, 2, 1024, 2048], P(None, None, 'gz', 'gy'), may hold values from 256 to 2048
- coupling: float32 [2], replicated, may hold values from 0.2 to 1.5
Outputs:
- stepped: float32 [2, 2, 1024, 2048], P(None, None, 'gz', 'gy')
The draws below stay inside these ranges and needn't reach their ends.
All inputs are finite; a program needn't handle non-finite values.
Results may differ from the reference program's by a relative error of at most 0.0018.
Values sent between devices are 32-bit elements; how exact they have to be, the bound alone decides.
No kernel may reach another device: no remote copies, remote signals or barrier semaphores. Data moves between devices by JAX's collectives and lax.ppermute only.
A program may use at most 128 MiB of HBM per device.

```python
import math
import jax
import jax.numpy as jnp
from jax import lax

NX = 2
NZ = 1024
NY = 2048


def draw_fields(key, part):
    rough_key, amp_key, phase_key = jax.random.split(key, 3)
    z_angle = jnp.arange(NZ, dtype=jnp.float32)[:, None] * (2.0 * math.pi / NZ)
    y_angle = jnp.arange(NY, dtype=jnp.float32)[None, :] * (2.0 * math.pi / NY)
    phases = jax.random.uniform(phase_key, (4, 2, NX, 1, 1), jnp.float32, -math.pi, math.pi)
    first_wave = jnp.cos(z_angle + phases[0]) * jnp.cos(y_angle + phases[1])
    second_wave = jnp.cos(2.0 * z_angle + phases[2]) * jnp.cos(2.0 * y_angle + phases[3])
    roughness = jnp.clip(jax.random.normal(rough_key, (2, NX, NZ, NY), jnp.float32), -4.0, 4.0)
    amplitude = jax.random.uniform(amp_key, (2, 2, NX, 1, 1), jnp.float32, 0.6, 1.6)
    return amplitude[0] * first_wave + amplitude[1] * second_wave + roughness


def block_scale(stream_key, extent, shards, smallest, high):
    factor_of = 1.0
    for axis_at, parts in shards:
        heights = jax.random.uniform(jax.random.fold_in(jax.random.fold_in(stream_key, 6), axis_at), (parts,), jnp.float32, smallest / len(shards), high / len(shards))
        factor_of = factor_of * jnp.repeat(jnp.exp(heights), extent[axis_at] // parts).reshape((-1,) + (1,) * (len(extent) - 1 - axis_at))
    return factor_of


def setup_inputs(seed: int = 0) -> dict:
    splits = jax.random.split(jax.random.key(seed), 6)
    return {
        "fields": draw_fields(jax.random.fold_in(splits[5], 71), 0),
        "cond_x": jnp.clip(jnp.exp(jax.random.uniform(splits[1], (2, NX), jnp.float32, math.log(0.05), math.log(0.4))), 0.05, 0.4),
        "cond_y": jnp.clip(jnp.exp(math.log(32768.0) - 2.0794415 * jax.random.uniform(splits[2], (2, NX, NZ, NY), jnp.float32) ** block_scale(splits[2], (2, NX, NZ, NY), ((2, 32), (3, 4)), -0.2, 0.2)), 4096.0, 32768.0),
        "cond_z": jnp.clip(jnp.exp(math.log(2048.0) - 2.0794415 * jax.random.uniform(splits[3], (2, NX, NZ, NY), jnp.float32) ** block_scale(splits[3], (2, NX, NZ, NY), ((2, 32), (3, 4)), -0.2, 0.2)), 256.0, 2048.0),
        "coupling": jnp.clip(jnp.exp(jax.random.uniform(splits[4], (NX,), jnp.float32, math.log(0.2), math.log(1.5))), 0.2, 1.5),
    }


implicit_share = 0.5

def neighbour_pair(values, line_axis):
    widths = [(1, 1) if dimension == line_axis else (0, 0) for dimension in range(values.ndim)]
    padded = jnp.pad(values, widths)
    length = values.shape[line_axis]
    upper = lax.slice_in_dim(padded, 2, length + 2, axis=line_axis)
    lower = lax.slice_in_dim(padded, 0, length, axis=line_axis)
    return (upper, lower)

def conduction(fields, upper, lower, conduct, cond_upper, cond_lower):
    face_upper = 0.5 * (conduct + cond_upper)
    face_lower = 0.5 * (conduct + cond_lower)
    flow = face_upper * (upper - fields) - face_lower * (fields - lower)
    return (flow, face_upper, face_lower)

def direction_flow(fields, conduct, line_axis):
    upper, lower = neighbour_pair(fields, line_axis)
    cond_upper, cond_lower = neighbour_pair(conduct, line_axis)
    return conduction(fields, upper, lower, conduct, cond_upper, cond_lower)

def layer_flow(fields, cond_x):
    upper, lower = neighbour_pair(fields, 1)
    cond_upper, cond_lower = neighbour_pair(cond_x, 1)
    face_upper = (0.5 * (cond_x + cond_upper))[:, :, None, None]
    face_lower = (0.5 * (cond_x + cond_lower))[:, :, None, None]
    return face_upper * (upper - fields) - face_lower * (fields - lower)

def solve_lines(rhs, face_upper, face_lower, line_axis):
    lower_diag = jnp.moveaxis(-implicit_share * face_lower, line_axis, -1)
    main_diag = jnp.moveaxis(1.0 + implicit_share * (face_upper + face_lower), line_axis, -1)
    upper_diag = jnp.moveaxis(-implicit_share * face_upper, line_axis, -1)
    lower_diag = lower_diag.at[..., 0].set(0.0)
    upper_diag = upper_diag.at[..., -1].set(0.0)
    right = jnp.moveaxis(rhs, line_axis, -1)[..., None]
    solution = lax.linalg.tridiagonal_solve(lower_diag, main_diag, upper_diag, right)[..., 0]
    return jnp.moveaxis(solution, -1, line_axis)

def reference(fields, cond_x, cond_y, cond_z, coupling):
    flow_x = layer_flow(fields, cond_x)
    flow_y, y_face_up, y_face_down = direction_flow(fields, cond_y, 3)
    flow_z, z_face_up, z_face_down = direction_flow(fields, cond_z, 2)
    explicit = fields + flow_x + flow_y + flow_z + coupling[None, :, None, None] * (fields[::-1] - fields)
    first_section = solve_lines(explicit - implicit_share * flow_y, y_face_up, y_face_down, 3)
    return solve_lines(first_section - implicit_share * flow_z, z_face_up, z_face_down, 2)
```

```python
import jax
import jax.numpy as jnp
from jax import lax
from jax.experimental import pallas as pl
from jax.experimental.pallas import tpu as pltpu
from jax.sharding import PartitionSpec as P

SUB = 8
F32 = jnp.float32
VMEM = pl.BlockSpec(memory_space=pltpu.VMEM)
SMEM = pl.BlockSpec(memory_space=pltpu.SMEM)


def strided(ref, start, count, stride):
    return ref[pl.ds(start, count, stride=stride), :]


def factor_kernel(
    cx, cp, u, ky, kz, gpy, gsy, ymat, gpz, gsz, zmat, r0, kt, zr, wa, wb, wc, wd, zz
):
    lines, length = ky.shape
    steps = length // SUB
    planes, depth = zmat.shape[1], lines // zmat.shape[1]
    kt[...] = ky[...].T
    first = strided(kt, 0, SUB, steps)
    here = first
    for t in range(steps):
        after = strided(kt, t + 1, SUB, steps) if t + 1 < steps else pltpu.roll(first, SUB - 1, 0)
        zr[t] = 4.0 / (here + after)
        here = after
    last = strided(kt, steps - 1, SUB, steps)
    row = lax.broadcasted_iota(jnp.int32, (SUB, lines), 0)
    one, zero = jnp.ones((SUB, lines), F32), jnp.zeros((SUB, lines), F32)
    aw, aj, bw, bj = one, zero, zero, one
    for t in range(steps):
        wa[t], wb[t] = aw, bw
        aj, bj = aj + aw, bj + bw
        aw, bw = aw + zr[t] * aj, bw + zr[t] * bj
    cw, cj, dw, dj = one, zero, zero, one
    for t in reversed(range(steps)):
        wc[t], wd[t] = cw, dw
        cj, dj = cj + cw, dj + dw
        z = zr[t - 1] if t else pltpu.roll(zr[steps - 1], 1, 0)
        cw, dw = cw + z * cj, dw + z * dj
    al, be, ga, de = one, zero, one, zero
    for j in range(SUB - 1):
        nal, nbe = pltpu.roll(aw * al + bw * be, 1, 0), pltpu.roll(aj * al + bj * be, 1, 0)
        al, be = jnp.where(row == j + 1, nal, al), jnp.where(row == j + 1, nbe, be)
        nga = pltpu.roll(cw * ga + dw * de, SUB - 1, 0)
        nde = pltpu.roll(cj * ga + dj * de, SUB - 1, 0)
        at = SUB - 2 - j
        ga, de = jnp.where(row == at, nga, ga), jnp.where(row == at, nde, de)
    iw = 1.0 / (aj * al + bj * be)[SUB - 1 :, :]
    iv = 1.0 / (cj * ga + dj * de)[:1, :]
    al, be, ga, de = al * iw, be * iw, ga * iv, de * iv
    for t in range(steps):
        gpy[t] = al * wa[t] + be * wb[t]
        gsy[t] = ga * wc[t] + de * wd[t]
    ymat[...] = jnp.zeros_like(ymat)
    ymat[2:3, :] = gsy[0][:1, :]
    ymat[3:4, :] = iw
    ymat[4:5, :] = gpy[steps - 1][SUB - 1 :, :]
    ymat[5:6, :] = first[:1, :]
    ymat[6:7, :] = last[SUB - 1 :, :]
    here = [kz[pl.ds(p * depth, 1), :] for p in range(planes)]
    here = jnp.concatenate(here, 0)
    for t in range(depth - 1):
        after = jnp.concatenate([kz[pl.ds(p * depth + t + 1, 1), :] for p in range(planes)], 0)
        zz[t] = 4.0 / (here + after)
        here = after
    w, j = jnp.ones_like(here), jnp.zeros_like(here)
    ws = []
    for t in range(depth):
        ws.append(w)
        j = j + w
        if t + 1 < depth:
            w = w + zz[t] * j
    ij = 1.0 / j
    for t in range(depth):
        g = ws[t] * ij
        for p in range(planes):
            gpz[pl.ds(p * depth + t, 1), :] = g[p : p + 1, :]
    zmat[1] = ij
    zmat[2] = ws[depth - 1] * ij
    w, j = jnp.ones_like(here), jnp.zeros_like(here)
    ws = []
    for t in reversed(range(depth)):
        ws.append(w)
        j = j + w
        if t:
            w = w + zz[t - 1] * j
    ij = 1.0 / j
    for t in range(depth):
        g = ws[depth - 1 - t] * ij
        for p in range(planes):
            gsz[pl.ds(p * depth + t, 1), :] = g[p : p + 1, :]
    zmat[0] = ws[depth - 1] * ij
    for f in range(2):
        for x in range(2):
            at = (f * 2 + x) * depth
            me = u[at : at + depth, :]
            beside = u[(f * 2 + 1 - x) * depth : (f * 2 + 2 - x) * depth, :]
            other = u[((1 - f) * 2 + x) * depth : ((1 - f) * 2 + x + 1) * depth, :]
            face = 0.5 * (cx[f, 0] + cx[f, 1])
            k = kz[at : at + depth, :]
            flux = 0.5 * (k[1:] + k[:-1]) * (me[1:] - me[:-1])
            none = jnp.zeros((1, length), F32)
            flow = jnp.concatenate([flux, none], 0) - jnp.concatenate([none, flux], 0)
            r0[at : at + depth, :] = (
                (2.0 - 0.5 * cx[f, x]) * me
                + face * (beside - me)
                + cp[x] * (other - me)
                + flow
            )


def y_local_kernel(r0, lo, hi, gpy, gsy, ymat, msg, vloc, rt, ss):
    steps, _, lines = gpy.shape
    length = steps * SUB
    planes = lo.shape[0]
    depth = lines // planes
    row = lax.broadcasted_iota(jnp.int32, (SUB, length), 0)
    parts = []
    for p in range(planes):
        at = p * depth
        top, mid, end = r0[at : at + SUB], r0[at + SUB : at + depth - SUB], r0[at + depth - SUB : at + depth]
        parts += [
            jnp.where(row == 0, top + lo[p : p + 1, :], top),
            mid,
            jnp.where(row == SUB - 1, end + hi[p : p + 1, :], end),
        ]
    rt[...] = jnp.concatenate(parts, 0).T
    s = jnp.zeros((SUB, lines), F32)
    for t in range(steps):
        s = s + gpy[t] * strided(rt, t, SUB, steps)
        ss[t] = s
    q = jnp.zeros((SUB, lines), F32)
    for t in reversed(range(steps)):
        vloc[t] = q
        q = q + gsy[t] * strided(rt, t, SUB, steps)
    srow = lax.broadcasted_iota(jnp.int32, (SUB, lines), 0)
    so, qo = jnp.zeros_like(s), jnp.zeros_like(q)
    for j in range(1, SUB):
        so = so + jnp.where(srow >= j, pltpu.roll(s, j, 0), 0.0)
        qo = qo + jnp.where(srow < SUB - j, pltpu.roll(q, SUB - j, 0), 0.0)
    msg[...] = ymat[...]
    msg[0:1, :] = (q + qo)[:1, :]
    msg[1:2, :] = (s + so)[SUB - 1 :, :]
    w = 1.0 / ymat[3:4, :]
    for t in range(steps):
        vloc[t] = gsy[t] * w * (ss[t] + so) + gpy[t] * w * (vloc[t] + qo)


def y_finish_kernel(me, m0, m1, m2, m3, vloc, gpy, gsy, u, gpz, gsz, rz, az, dz, buf, vt):
    steps, _, lines = gpy.shape
    planes = az.shape[0]
    depth = lines // planes
    got = (m0, m1, m2, m3)
    mine = me[0]
    for k in range(4):
        buf[lax.rem(mine + 4 - k, 4)] = got[k][...]
    seg = []
    for j in range(4):
        s = buf[j]
        seg.append([s[i : i + 1, :] for i in range(7)])
    zero = jnp.zeros((1, lines), F32)
    gap = [4.0 / (seg[j][6] + seg[j + 1][5]) for j in range(3)]
    e, r = zero, 4.0 / seg[0][5]
    el, rl = e, r
    for j in range(3):
        a, d, b, c, f = seg[j][:5]
        inv = 1.0 / (r + b)
        e, r = d + c * (e - a) * inv, f - c * c * inv + gap[j]
        el, rl = jnp.where(mine == j + 1, e, el), jnp.where(mine == j + 1, r, rl)
    e, r = zero, 4.0 / seg[3][6]
    er, rr = e, r
    for j in (3, 2, 1):
        a, d, b, c, f = seg[j][:5]
        inv = 1.0 / (r + f)
        e, r = a + c * (e - d) * inv, b - c * c * inv + gap[j - 1]
        er, rr = jnp.where(mine == j - 1, e, er), jnp.where(mine == j - 1, r, rr)
    a, d, b, c, f = [m0[i : i + 1, :] for i in range(5)]
    left, right = b + rl, f + rr
    inv = 1.0 / (left * right - c * c)
    ql = ((el - a) * right - c * (er - d)) * inv
    qr = ((er - d) * left - c * (el - a)) * inv
    for t in range(steps):
        vt[pl.ds(t, SUB, stride=steps), :] = vloc[t] + gsy[t] * ql + gpy[t] * qr
    v = vt[...].T
    for p in range(planes):
        at = p * depth
        r = v[at : at + depth, :] - 2.0 * u[at : at + depth, :]
        rz[at : at + depth, :] = r
        az[p : p + 1, :] = jnp.sum(gsz[at : at + depth, :] * r, axis=0, keepdims=True)
        dz[p : p + 1, :] = jnp.sum(gpz[at : at + depth, :] * r, axis=0, keepdims=True)


def z_local_kernel(u, rz, gpz, gsz, cross, out):
    planes, length = cross.shape
    depth = rz.shape[0] // planes
    for p in range(planes):
        w = 1.0 / cross[p : p + 1, :]
        s = jnp.zeros((1, length), F32)
        ss = []
        for t in range(depth):
            at = pl.ds(p * depth + t, 1)
            s = s + gpz[at, :] * rz[at, :]
            ss.append(s)
        q = jnp.zeros((1, length), F32)
        for t in reversed(range(depth)):
            at = pl.ds(p * depth + t, 1)
            out[at, :] = u[at, :] + w * (gsz[at, :] * ss[t] + gpz[at, :] * q)
            q = q + gsz[at, :] * rz[at, :]


def call(kernel, outs, scratch, cost, in_specs, *args):
    return pl.pallas_call(
        kernel,
        out_shape=[jax.ShapeDtypeStruct(s, F32) for s in outs],
        in_specs=in_specs,
        out_specs=[VMEM] * len(outs),
        scratch_shapes=[pltpu.VMEM(s, F32) for s in scratch],
        compiler_params=pltpu.CompilerParams(vmem_limit_bytes=40 * 1024 * 1024),
        cost_estimate=pl.CostEstimate(flops=cost, bytes_accessed=cost // 4, transcendentals=0),
    )(*args)


def join(s, t):
    a1, d1, b1, e1, f1 = s
    a2, d2, b2, e2, f2 = t
    inv = 1.0 / (f1 + b2)
    jump = (a2 - d1) * inv
    cross = e1 * inv
    return (
        a1 + e1 * jump,
        d2 - e2 * jump,
        b1 - e1 * cross,
        e2 * cross,
        f2 - e2 * e2 * inv,
    )


def middle(s, t, ql, qr):
    return (t[0] - s[1] + t[3] * qr - s[3] * ql) / (s[4] + t[2])


def ring(value, shift_of, position):
    got = [value] + [lax.ppermute(value, "gz", shift_of(k)) for k in (1, 2, 3)]
    ordered = []
    for j in range(4):
        pick = got[0]
        for k in (1, 2, 3):
            pick = jnp.where(position == (j + k) % 4, got[k], pick)
        ordered.append(tuple(pick[i] for i in range(5)))
    return ordered


def around_y(k):
    return [(i, (i // 8) * 8 + ((i // 2 % 4 + k) % 4) * 2 + i % 2) for i in range(32)]


def around_x(k):
    return [(i, ((i // 8 + k) % 4) * 8 + i % 8) for i in range(32)]


def shards(fields, cond_x, cond_y, cond_z, coupling):
    nf, nx, nz, ny = fields.shape
    planes, lines = nf * nx, nf * nx * nz
    u, ky, kz = (a.reshape(lines, ny) for a in (fields, cond_y, cond_z))
    u3, kz3 = u.reshape(planes, nz, ny), kz.reshape(planes, nz, ny)
    iy, iz = lax.axis_index("gy"), lax.axis_index("gz")
    peers = lax.axis_size("gz")
    low = jnp.stack([u3[:, 0], kz3[:, 0]])
    high = jnp.stack([u3[:, -1], kz3[:, -1]])
    below = lax.ppermute(high, "gz", [(i, (i + 1) % peers) for i in range(peers)])
    above = lax.ppermute(low, "gz", [(i, (i - 1) % peers) for i in range(peers)])
    steps = ny // SUB
    tall = (steps, SUB, lines)
    gpy, gsy, ymat, gpz, gsz, zmat, r0 = call(
        factor_kernel,
        [tall, tall, (8, lines), (lines, ny), (lines, ny), (3, planes, ny), (lines, ny)],
        [(ny, lines)] + [tall] * 5 + [(nz, planes, ny)],
        4_000_000,
        [SMEM, SMEM, VMEM, VMEM, VMEM],
        cond_x, coupling, u, ky, kz,
    )
    below = jnp.where(iz == 0, 0.0, below)
    above = jnp.where(iz == peers - 1, 0.0, above)
    lo = 0.5 * (below[1] + low[1]) * (below[0] - low[0])
    hi = 0.5 * (above[1] + high[1]) * (above[0] - high[0])
    msg, vloc = call(
        y_local_kernel, [(8, lines), tall], [(ny, lines), tall], 2_000_000, [VMEM] * 6,
        r0, lo, hi, gpy, gsy, ymat,
    )
    others = [lax.ppermute(msg, "gy", [(i, (i + k) % 4) for i in range(4)]) for k in (1, 2, 3)]
    rz, az, dz = call(
        y_finish_kernel,
        [(lines, ny), (planes, ny), (planes, ny)],
        [(4, 8, lines), (ny, lines)],
        1_000_000,
        [SMEM] + [VMEM] * 10,
        iy.reshape(1).astype(jnp.int32), msg, *others, vloc, gpy, gsy, u, gpz, gsz,
    )
    b = zmat[0] + jnp.where(iz == 0, 4.0 / low[1], 0.0)
    f = zmat[2] + 4.0 / (above[1] + high[1])
    own = jnp.stack([az, dz, b, zmat[1], f])
    peer = lax.ppermute(own, "gz", [(i, i ^ 1) for i in range(peers)])
    [local] = call(
        z_local_kernel, [(lines, ny)], [], 1_000_000, [VMEM] * 5, u, rz, gpz, gsz, zmat[1]
    )
    core, at_y, at_x = iz % 2, iz // 2 % 4, iz // 8
    first, second = jnp.where(core == 0, own, peer), jnp.where(core == 0, peer, own)
    chip = jnp.stack(join(first, second))
    column = ring(chip, around_y, at_y)
    lower, upper = join(column[0], column[1]), join(column[2], column[3])
    plane = jnp.stack(join(lower, upper))
    whole = ring(plane, around_x, at_x)
    halves = join(whole[0], whole[1]), join(whole[2], whole[3])

    (a1, d1, b1, e1, f1), (a2, d2, b2, e2, f2) = halves
    a, d, b, e, f = join(*halves)
    inv = 1.0 / (b * f - e * e)
    ql, qr = (e * d - f * a) * inv, (e * a - b * d) * inv

    def descend(level, position, ql, qr):
        for bit in range(len(level).bit_length() - 2, -1, -1):
            groups = list(level)
            for _ in range(bit):
                groups = [join(groups[i], groups[i + 1]) for i in range(0, len(groups), 2)]
            n = len(groups)
            span = position // (2**bit)
            pair = [
                tuple(sum_pick(groups, span // 2 * 2 + side, n, i) for i in range(5))
                for side in (0, 1)
            ]
            q = middle(pair[0], pair[1], ql, qr)
            up = span % 2 == 1
            ql, qr = jnp.where(up, -q, ql), jnp.where(up, qr, q)
        return ql, qr

    def sum_pick(groups, index, n, i):
        pick = groups[0][i]
        for j in range(1, n):
            pick = jnp.where(index == j, groups[j][i], pick)
        return pick

    ql, qr = descend(whole, at_x, ql, qr)
    ql, qr = descend(column, at_y, ql, qr)
    ql, qr = descend([tuple(first), tuple(second)], core, ql, qr)
    shape = (planes, nz, ny)
    out = (
        local.reshape(shape)
        + gsz.reshape(shape) * ql[:, None, :]
        + gpz.reshape(shape) * qr[:, None, :]
    )
    return out.reshape(fields.shape)


def solution(mesh):
    block = P(None, None, "gz", "gy")
    return jax.shard_map(
        shards,
        mesh=mesh,
        in_specs=(block, P(), block, block, P()),
        out_specs=block,
        check_vma=False,
    )
```

```python
import functools

import jax
import jax.numpy as jnp
from jax import lax
from jax.experimental import pallas as pl
from jax.experimental.pallas import tpu as pltpu
from jax.sharding import PartitionSpec as P

SUB = 8
F32 = jnp.float32
VMEM = pl.BlockSpec(memory_space=pltpu.VMEM)
SMEM = pl.BlockSpec(memory_space=pltpu.SMEM)


def strided(ref, start, count, stride):
    return ref[pl.ds(start, count, stride=stride), :]


def load_kernel(uh, kyh, kzh, u, ky, kz, low, high, inner, outer, sem):
    copies = [
        pltpu.make_async_copy(src, dst, sem.at[i])
        for i, (src, dst) in enumerate(((uh, u), (kzh, kz), (kyh, ky)))
    ]
    for copy in copies:
        copy.start()
    planes = low.shape[1]
    depth = u.shape[0] // planes
    even = lax.axis_index("gz") % 2 == 0
    for i, array in enumerate((u, kz)):
        copies[i].wait()
        for p in range(planes):
            at = p * depth
            bottom, top = array[at : at + 1, :], array[at + depth - 1 : at + depth, :]
            low[i, p : p + 1, :] = bottom
            high[i, p : p + 1, :] = top
            inner[i, p : p + 1, :] = jnp.where(even, top, bottom)
            outer[i, p : p + 1, :] = jnp.where(even, bottom, top)
    copies[2].wait()


def factor_kernel(
    cxh, cph, u, ky, kz, gpy, gsy, ymat, gpz, gsz, zmat, r0, kt, zr, wa, wb, wc, wd, zz, cx, cp, sem
):
    small = [pltpu.make_async_copy(cxh, cx, sem.at[0]), pltpu.make_async_copy(cph, cp, sem.at[1])]
    for copy in small:
        copy.start()
    lines, length = ky.shape
    steps = length // SUB
    planes, depth = zmat.shape[1], lines // zmat.shape[1]
    kt[...] = ky[...].T
    first = strided(kt, 0, SUB, steps)
    here = first
    for t in range(steps):
        after = strided(kt, t + 1, SUB, steps) if t + 1 < steps else pltpu.roll(first, SUB - 1, 0)
        zr[t] = 4.0 / (here + after)
        here = after
    last = strided(kt, steps - 1, SUB, steps)
    row = lax.broadcasted_iota(jnp.int32, (SUB, lines), 0)
    one, zero = jnp.ones((SUB, lines), F32), jnp.zeros((SUB, lines), F32)
    aw, aj, bw, bj = one, zero, zero, one
    for t in range(steps):
        wa[t], wb[t] = aw, bw
        aj, bj = aj + aw, bj + bw
        aw, bw = aw + zr[t] * aj, bw + zr[t] * bj
    cw, cj, dw, dj = one, zero, zero, one
    for t in reversed(range(steps)):
        wc[t], wd[t] = cw, dw
        cj, dj = cj + cw, dj + dw
        z = zr[t - 1] if t else pltpu.roll(zr[steps - 1], 1, 0)
        cw, dw = cw + z * cj, dw + z * dj
    al, be, ga, de = one, zero, one, zero
    for j in range(SUB - 1):
        nal, nbe = pltpu.roll(aw * al + bw * be, 1, 0), pltpu.roll(aj * al + bj * be, 1, 0)
        al, be = jnp.where(row == j + 1, nal, al), jnp.where(row == j + 1, nbe, be)
        nga = pltpu.roll(cw * ga + dw * de, SUB - 1, 0)
        nde = pltpu.roll(cj * ga + dj * de, SUB - 1, 0)
        at = SUB - 2 - j
        ga, de = jnp.where(row == at, nga, ga), jnp.where(row == at, nde, de)
    iw = 1.0 / (aj * al + bj * be)[SUB - 1 :, :]
    iv = 1.0 / (cj * ga + dj * de)[:1, :]
    al, be, ga, de = al * iw, be * iw, ga * iv, de * iv
    for t in range(steps):
        gpy[t] = al * wa[t] + be * wb[t]
        gsy[t] = ga * wc[t] + de * wd[t]
    ymat[...] = jnp.zeros_like(ymat)
    ymat[2:3, :] = gsy[0][:1, :]
    ymat[3:4, :] = iw
    ymat[4:5, :] = gpy[steps - 1][SUB - 1 :, :]
    ymat[5:6, :] = first[:1, :]
    ymat[6:7, :] = last[SUB - 1 :, :]
    here = [kz[pl.ds(p * depth, 1), :] for p in range(planes)]
    here = jnp.concatenate(here, 0)
    for t in range(depth - 1):
        after = jnp.concatenate([kz[pl.ds(p * depth + t + 1, 1), :] for p in range(planes)], 0)
        zz[t] = 4.0 / (here + after)
        here = after
    w, j = jnp.ones_like(here), jnp.zeros_like(here)
    ws = []
    for t in range(depth):
        ws.append(w)
        j = j + w
        if t + 1 < depth:
            w = w + zz[t] * j
    ij = 1.0 / j
    for t in range(depth):
        g = ws[t] * ij
        for p in range(planes):
            gpz[pl.ds(p * depth + t, 1), :] = g[p : p + 1, :]
    zmat[1] = ij
    zmat[2] = ws[depth - 1] * ij
    w, j = jnp.ones_like(here), jnp.zeros_like(here)
    ws = []
    for t in reversed(range(depth)):
        ws.append(w)
        j = j + w
        if t:
            w = w + zz[t - 1] * j
    ij = 1.0 / j
    for t in range(depth):
        g = ws[depth - 1 - t] * ij
        for p in range(planes):
            gsz[pl.ds(p * depth + t, 1), :] = g[p : p + 1, :]
    zmat[0] = ws[depth - 1] * ij
    for copy in small:
        copy.wait()
    for f in range(2):
        for x in range(2):
            at = (f * 2 + x) * depth
            me = u[at : at + depth, :]
            beside = u[(f * 2 + 1 - x) * depth : (f * 2 + 2 - x) * depth, :]
            other = u[((1 - f) * 2 + x) * depth : ((1 - f) * 2 + x + 1) * depth, :]
            face = 0.5 * (cx[f, 0] + cx[f, 1])
            k = kz[at : at + depth, :]
            flux = 0.5 * (k[1:] + k[:-1]) * (me[1:] - me[:-1])
            none = jnp.zeros((1, length), F32)
            flow = jnp.concatenate([flux, none], 0) - jnp.concatenate([none, flux], 0)
            r0[at : at + depth, :] = (
                (2.0 - 0.5 * cx[f, x]) * me
                + face * (beside - me)
                + cp[x] * (other - me)
                + flow
            )


def y_ends_kernel(peers, r0, low, high, inner, outer, gpy, gsy, ymat, msg, rt, ss, qq):
    steps, _, lines = gpy.shape
    length = steps * SUB
    planes = low.shape[1]
    depth = lines // planes
    under = jnp.where(lax.axis_index("gz") > 0, 1.0, 0.0)
    over = jnp.where(lax.axis_index("gz") < peers - 1, 1.0, 0.0)
    even = lax.axis_index("gz") % 2 == 0
    below = [jnp.where(even, outer[i], inner[i]) * under for i in range(2)]
    above = [jnp.where(even, inner[i], outer[i]) * over for i in range(2)]
    lo = 0.5 * (below[1] + low[1]) * (below[0] - low[0])
    hi = 0.5 * (above[1] + high[1]) * (above[0] - high[0])
    row = lax.broadcasted_iota(jnp.int32, (SUB, length), 0)
    parts = []
    for p in range(planes):
        i = p * depth
        top, mid, end = r0[i : i + SUB], r0[i + SUB : i + depth - SUB], r0[i + depth - SUB : i + depth]
        parts += [
            jnp.where(row == 0, top + lo[p : p + 1, :], top),
            mid,
            jnp.where(row == SUB - 1, end + hi[p : p + 1, :], end),
        ]
    rt[...] = jnp.concatenate(parts, 0).T
    s = jnp.zeros((SUB, lines), F32)
    q = jnp.zeros((SUB, lines), F32)
    for t in range(steps):
        back = steps - 1 - t
        s = s + gpy[t] * strided(rt, t, SUB, steps)
        ss[t] = s
        qq[back] = q
        q = q + gsy[back] * strided(rt, back, SUB, steps)
    msg[...] = ymat[...]
    msg[0:1, :] = jnp.sum(q, axis=0, keepdims=True)
    msg[1:2, :] = jnp.sum(s, axis=0, keepdims=True)


def y_local_kernel(peers, low, high, inner, outer, zmat, rt, ss, qq, gpy, gsy, ymat, vloc, zends):
    steps, _, lines = gpy.shape
    s = ss[steps - 1]
    q = qq[0] + gsy[0] * strided(rt, 0, SUB, steps)
    row = lax.broadcasted_iota(jnp.int32, (SUB, lines), 0)
    so, qo = jnp.zeros_like(s), jnp.zeros_like(q)
    for j in range(1, SUB):
        so = so + jnp.where(row >= j, pltpu.roll(s, j, 0), 0.0)
        qo = qo + jnp.where(row < SUB - j, pltpu.roll(q, SUB - j, 0), 0.0)
    w = 1.0 / ymat[3:4, :]
    for t in range(steps):
        vloc[t] = gsy[t] * w * (ss[t] + so) + gpy[t] * w * (qq[t] + qo)
    under = jnp.where(lax.axis_index("gz") > 0, 0.0, 1.0)
    over = jnp.where(lax.axis_index("gz") < peers - 1, 1.0, 0.0)
    zends[0] = zmat[0] + under * 4.0 / low[1]
    zends[1] = zmat[1]
    above = jnp.where(lax.axis_index("gz") % 2 == 0, inner[1], outer[1])
    zends[2] = zmat[2] + 4.0 / (above * over + high[1])


def y_finish_kernel(m0, m1, m2, m3, vloc, gpy, gsy, u, gpz, gsz, zends, rz, own, buf, vt):
    steps, _, lines = gpy.shape
    planes = own.shape[1]
    depth = lines // planes
    got = (m0, m1, m2, m3)
    mine = lax.axis_index("gy")
    for k in range(4):
        buf[mine ^ k] = got[k][...]
    seg = []
    for j in range(4):
        s = buf[j]
        seg.append([s[i : i + 1, :] for i in range(7)])
    zero = jnp.zeros((1, lines), F32)
    gap = [4.0 / (seg[j][6] + seg[j + 1][5]) for j in range(3)]
    e, r = zero, 4.0 / seg[0][5]
    el, rl = e, r
    for j in range(3):
        a, d, b, c, f = seg[j][:5]
        inv = 1.0 / (r + b)
        e, r = d + c * (e - a) * inv, f - c * c * inv + gap[j]
        el, rl = jnp.where(mine == j + 1, e, el), jnp.where(mine == j + 1, r, rl)
    e, r = zero, 4.0 / seg[3][6]
    er, rr = e, r
    for j in (3, 2, 1):
        a, d, b, c, f = seg[j][:5]
        inv = 1.0 / (r + f)
        e, r = a + c * (e - d) * inv, b - c * c * inv + gap[j - 1]
        er, rr = jnp.where(mine == j - 1, e, er), jnp.where(mine == j - 1, r, rr)
    a, d, b, c, f = [m0[i : i + 1, :] for i in range(5)]
    left, right = b + rl, f + rr
    inv = 1.0 / (left * right - c * c)
    ql = ((el - a) * right - c * (er - d)) * inv
    qr = ((er - d) * left - c * (el - a)) * inv
    for t in range(steps):
        vt[pl.ds(t, SUB, stride=steps), :] = vloc[t] + gsy[t] * ql + gpy[t] * qr
    v = vt[...].T
    for p in range(planes):
        i = p * depth
        r = v[i : i + depth, :] - 2.0 * u[i : i + depth, :]
        rz[i : i + depth, :] = r
        own[0, p : p + 1, :] = jnp.sum(gsz[i : i + depth, :] * r, axis=0, keepdims=True)
        own[1, p : p + 1, :] = jnp.sum(gpz[i : i + depth, :] * r, axis=0, keepdims=True)
    for i in range(3):
        own[i + 2] = zends[i]


def z_local_kernel(u, rz, gpz, gsz, zmat, out):
    _, planes, length = zmat.shape
    depth = rz.shape[0] // planes
    for p in range(planes):
        w = 1.0 / zmat[1, p : p + 1, :]
        s = jnp.zeros((1, length), F32)
        ss = []
        for t in range(depth):
            at = pl.ds(p * depth + t, 1)
            s = s + gpz[at, :] * rz[at, :]
            ss.append(s)
        q = jnp.zeros((1, length), F32)
        for t in reversed(range(depth)):
            at = pl.ds(p * depth + t, 1)
            out[at, :] = u[at, :] + w * (gsz[at, :] * ss[t] + gpz[at, :] * q)
            q = q + gsz[at, :] * rz[at, :]


def call(kernel, outs, scratch, cost, in_specs, *args, vmem=32):
    return pl.pallas_call(
        kernel,
        out_shape=[jax.ShapeDtypeStruct(s, F32) for s in outs],
        in_specs=in_specs,
        out_specs=[VMEM] * len(outs),
        scratch_shapes=[pltpu.VMEM(s, F32) if isinstance(s, tuple) else s for s in scratch],
        compiler_params=pltpu.CompilerParams(vmem_limit_bytes=int(vmem * 2**20)),
        cost_estimate=pl.CostEstimate(flops=cost, bytes_accessed=cost // 4, transcendentals=0),
    )(*args)


def join(s, t):
    a1, d1, b1, e1, f1 = s
    a2, d2, b2, e2, f2 = t
    inv = 1.0 / (f1 + b2)
    jump = (a2 - d1) * inv
    cross = e1 * inv
    return (
        a1 + e1 * jump,
        d2 - e2 * jump,
        b1 - e1 * cross,
        e2 * cross,
        f2 - e2 * e2 * inv,
    )


def middle(s, t, ql, qr):
    return (t[0] - s[1] + t[3] * qr - s[3] * ql) / (s[4] + t[2])


def parts_of(ref):
    return tuple(ref[i] for i in range(5))


def choose(flag, s, t):
    return tuple(jnp.where(flag, a, b) for a, b in zip(s, t))


def put(ref, value):
    for i in range(5):
        ref[i] = value[i]


def core_kernel(own, peer, chip):
    lower = lax.axis_index("gz") % 2 == 0
    mine, theirs = parts_of(own), parts_of(peer)
    put(chip, join(choose(lower, mine, theirs), choose(lower, theirs, mine)))


def ring_kernel(position, m0, m1, m2, m3, plane, buf):
    mine = position(lax.axis_index("gz"))
    for k, got in enumerate((m0, m1, m2, m3)):
        buf[mine ^ k] = got[...]
    s = [parts_of(buf.at[j]) for j in range(4)]
    put(plane, join(join(s[0], s[1]), join(s[2], s[3])))


def descend(mine, s, ql, qr):
    lower, upper = join(s[0], s[1]), join(s[2], s[3])
    q = middle(lower, upper, ql, qr)
    up = mine // 2 == 1
    ql, qr = jnp.where(up, -q, ql), jnp.where(up, qr, q)
    q = middle(choose(up, s[2], s[0]), choose(up, s[3], s[1]), ql, qr)
    up = mine % 2 == 1
    return jnp.where(up, -q, ql), jnp.where(up, qr, q)


def finish_kernel(
    own, peer, c0, c1, c2, c3, p0, p1, p2, p3, local, gpz, gsz, out, cbuf, pbuf
):
    iy, ix = position_y(lax.axis_index("gz")), position_x(lax.axis_index("gz"))
    for k, (c, p) in enumerate(((c0, p0), (c1, p1), (c2, p2), (c3, p3))):
        cbuf[iy ^ k] = c[...]
        pbuf[ix ^ k] = p[...]
    column = [parts_of(cbuf.at[j]) for j in range(4)]
    whole = [parts_of(pbuf.at[j]) for j in range(4)]
    a, d, b, e, f = join(join(whole[0], whole[1]), join(whole[2], whole[3]))
    inv = 1.0 / (b * f - e * e)
    ql, qr = (e * d - f * a) * inv, (e * a - b * d) * inv
    ql, qr = descend(ix, whole, ql, qr)
    ql, qr = descend(iy, column, ql, qr)
    lower = lax.axis_index("gz") % 2 == 0
    mine, theirs = parts_of(own), parts_of(peer)
    q = middle(choose(lower, mine, theirs), choose(lower, theirs, mine), ql, qr)
    ql, qr = jnp.where(lower, ql, -q), jnp.where(lower, q, qr)
    planes = ql.shape[0]
    depth = out.shape[0] // planes
    for p in range(planes):
        i = p * depth
        out[i : i + depth, :] = (
            local[i : i + depth, :]
            + gsz[i : i + depth, :] * ql[p : p + 1, :]
            + gpz[i : i + depth, :] * qr[p : p + 1, :]
        )


def position_y(z):
    return z // 2 % 4


def position_x(z):
    return z // 8


def partners(value, axis, count, unit):
    return [
        lax.ppermute(value, axis, [(i, i ^ (k * unit)) for i in range(count)]) for k in (1, 2, 3)
    ]


def shards(fields, cond_x, cond_y, cond_z, coupling):
    nf, nx, nz, ny = fields.shape
    planes, lines = nf * nx, nf * nx * nz
    peers = lax.axis_size("gz")
    steps = ny // SUB
    tall, flat, face, ends = (steps, SUB, lines), (lines, ny), (planes, ny), (5, planes, ny)
    hbm = pl.BlockSpec(memory_space=pltpu.HBM)
    dma = pltpu.SemaphoreType.DMA
    u, ky, kz, low, high, inner, outer = call(
        load_kernel, [flat] * 3 + [(2, *face)] * 4, [dma((3,))], 100_000, [hbm] * 3,
        fields.reshape(flat), cond_y.reshape(flat), cond_z.reshape(flat), vmem=53,
    )
    across = [pair for i in range(1, peers - 1, 2) for pair in ((i, i + 1), (i + 1, i))]
    outer = lax.ppermute(outer, "gz", across)
    inner = lax.ppermute(inner, "gz", [(i, i ^ 1) for i in range(peers)])
    gpy, gsy, ymat, gpz, gsz, zmat, r0 = call(
        factor_kernel,
        [tall, tall, (8, lines), flat, flat, (3, *face), flat],
        [(ny, lines)] + [tall] * 5 + [(nz, *face), pltpu.SMEM(cond_x.shape, F32), pltpu.SMEM(coupling.shape, F32), dma((2,))],
        4_000_000,
        [hbm, hbm, VMEM, VMEM, VMEM],
        cond_x, coupling, u, ky, kz,
    )
    msg, rt, ss, qq = call(
        functools.partial(y_ends_kernel, peers), [(8, lines), (ny, lines), tall, tall], [], 1_000_000, [VMEM] * 8,
        r0, low, high, inner, outer, gpy, gsy, ymat,
    )
    others = partners(msg, "gy", 4, 1)
    vloc, zends = call(
        functools.partial(y_local_kernel, peers), [tall, (3, *face)], [], 1_000_000, [VMEM] * 11,
        low, high, inner, outer, zmat, rt, ss, qq, gpy, gsy, ymat,
    )
    rz, own = call(
        y_finish_kernel, [flat, ends], [(4, 8, lines), (ny, lines)], 1_000_000, [VMEM] * 11,
        msg, *others, vloc, gpy, gsy, u, gpz, gsz, zends,
    )
    peer = lax.ppermute(own, "gz", [(i, i ^ 1) for i in range(peers)])
    [local] = call(z_local_kernel, [flat], [], 1_000_000, [VMEM] * 5, u, rz, gpz, gsz, zmat)
    [chip] = call(core_kernel, [ends], [], 50_000, [VMEM] * 2, own, peer)
    column = [chip] + partners(chip, "gz", peers, 2)
    [plane] = call(
        functools.partial(ring_kernel, position_y), [ends], [(4, *ends)], 50_000,
        [VMEM] * 4, *column,
    )
    whole = [plane] + partners(plane, "gz", peers, 8)
    [out] = call(
        finish_kernel, [flat], [(4, *ends), (4, *ends)], 1_000_000, [VMEM] * 13,
        own, peer, *column, *whole, local, gpz, gsz,
    )
    return out.reshape(fields.shape)


def solution(mesh):
    block = P(None, None, "gz", "gy")
    return jax.shard_map(
        shards,
        mesh=mesh,
        in_specs=(block, P(), block, block, P()),
        out_specs=block,
        check_vma=False,
    )
```

```python
import functools

import jax
import jax.numpy as jnp
from jax import lax
from jax.experimental import pallas as pl
from jax.experimental.pallas import tpu as pltpu
from jax.sharding import PartitionSpec as P

SUB = 8
F32 = jnp.float32
VMEM = pl.BlockSpec(memory_space=pltpu.VMEM)
SMEM = pl.BlockSpec(memory_space=pltpu.SMEM)


def strided(ref, start, count, stride):
    return ref[pl.ds(start, count, stride=stride), :]


def load_kernel(uh, kyh, kzh, u, ky, kz, low, high, inner, outer, sem):
    copies = [
        pltpu.make_async_copy(src, dst, sem.at[i])
        for i, (src, dst) in enumerate(((uh, u), (kzh, kz), (kyh, ky)))
    ]
    for copy in copies:
        copy.start()
    planes = low.shape[1]
    depth = u.shape[0] // planes
    even = lax.axis_index("gz") % 2 == 0
    for i, array in enumerate((u, kz)):
        copies[i].wait()
        for p in range(planes):
            at = p * depth
            bottom, top = array[at : at + 1, :], array[at + depth - 1 : at + depth, :]
            low[i, p : p + 1, :] = bottom
            high[i, p : p + 1, :] = top
            inner[i, p : p + 1, :] = jnp.where(even, top, bottom)
            outer[i, p : p + 1, :] = jnp.where(even, bottom, top)
    copies[2].wait()


def factor_kernel(
    cx, cp, u, ky, kz, gpy, gsy, ymat, gpz, gsz, zmat, r0, kt, zr, wa, wb, wc, wd, zz
):
    lines, length = ky.shape
    steps = length // SUB
    planes, depth = zmat.shape[1], lines // zmat.shape[1]
    kt[...] = ky[...].T
    first = strided(kt, 0, SUB, steps)
    here = first
    for t in range(steps):
        after = strided(kt, t + 1, SUB, steps) if t + 1 < steps else pltpu.roll(first, SUB - 1, 0)
        zr[t] = 4.0 / (here + after)
        here = after
    last = strided(kt, steps - 1, SUB, steps)
    row = lax.broadcasted_iota(jnp.int32, (SUB, lines), 0)
    one, zero = jnp.ones((SUB, lines), F32), jnp.zeros((SUB, lines), F32)
    aw, aj, bw, bj = one, zero, zero, one
    for t in range(steps):
        wa[t], wb[t] = aw, bw
        aj, bj = aj + aw, bj + bw
        aw, bw = aw + zr[t] * aj, bw + zr[t] * bj
    cw, cj, dw, dj = one, zero, zero, one
    for t in reversed(range(steps)):
        wc[t], wd[t] = cw, dw
        cj, dj = cj + cw, dj + dw
        z = zr[t - 1] if t else pltpu.roll(zr[steps - 1], 1, 0)
        cw, dw = cw + z * cj, dw + z * dj
    al, be, ga, de = one, zero, one, zero
    for j in range(SUB - 1):
        nal, nbe = pltpu.roll(aw * al + bw * be, 1, 0), pltpu.roll(aj * al + bj * be, 1, 0)
        al, be = jnp.where(row == j + 1, nal, al), jnp.where(row == j + 1, nbe, be)
        nga = pltpu.roll(cw * ga + dw * de, SUB - 1, 0)
        nde = pltpu.roll(cj * ga + dj * de, SUB - 1, 0)
        at = SUB - 2 - j
        ga, de = jnp.where(row == at, nga, ga), jnp.where(row == at, nde, de)
    iw = 1.0 / (aj * al + bj * be)[SUB - 1 :, :]
    iv = 1.0 / (cj * ga + dj * de)[:1, :]
    al, be, ga, de = al * iw, be * iw, ga * iv, de * iv
    for t in range(steps):
        gpy[t] = al * wa[t] + be * wb[t]
        gsy[t] = ga * wc[t] + de * wd[t]
    ymat[...] = jnp.zeros_like(ymat)
    ymat[2:3, :] = gsy[0][:1, :]
    ymat[3:4, :] = iw
    ymat[4:5, :] = gpy[steps - 1][SUB - 1 :, :]
    ymat[5:6, :] = first[:1, :]
    ymat[6:7, :] = last[SUB - 1 :, :]
    here = [kz[pl.ds(p * depth, 1), :] for p in range(planes)]
    here = jnp.concatenate(here, 0)
    for t in range(depth - 1):
        after = jnp.concatenate([kz[pl.ds(p * depth + t + 1, 1), :] for p in range(planes)], 0)
        zz[t] = 4.0 / (here + after)
        here = after
    w, j = jnp.ones_like(here), jnp.zeros_like(here)
    ws = []
    for t in range(depth):
        ws.append(w)
        j = j + w
        if t + 1 < depth:
            w = w + zz[t] * j
    ij = 1.0 / j
    for t in range(depth):
        g = ws[t] * ij
        for p in range(planes):
            gpz[pl.ds(p * depth + t, 1), :] = g[p : p + 1, :]
    zmat[1] = ij
    zmat[2] = ws[depth - 1] * ij
    w, j = jnp.ones_like(here), jnp.zeros_like(here)
    ws = []
    for t in reversed(range(depth)):
        ws.append(w)
        j = j + w
        if t:
            w = w + zz[t - 1] * j
    ij = 1.0 / j
    for t in range(depth):
        g = ws[depth - 1 - t] * ij
        for p in range(planes):
            gsz[pl.ds(p * depth + t, 1), :] = g[p : p + 1, :]
    zmat[0] = ws[depth - 1] * ij
    for f in range(2):
        for x in range(2):
            at = (f * 2 + x) * depth
            me = u[at : at + depth, :]
            beside = u[(f * 2 + 1 - x) * depth : (f * 2 + 2 - x) * depth, :]
            other = u[((1 - f) * 2 + x) * depth : ((1 - f) * 2 + x + 1) * depth, :]
            face = 0.5 * (cx[f : f + 1, 0:1] + cx[f : f + 1, 1:2])
            k = kz[at : at + depth, :]
            flux = 0.5 * (k[1:] + k[:-1]) * (me[1:] - me[:-1])
            none = jnp.zeros((1, length), F32)
            flow = jnp.concatenate([flux, none], 0) - jnp.concatenate([none, flux], 0)
            r0[at : at + depth, :] = (
                (2.0 - 0.5 * cx[f : f + 1, x : x + 1]) * me
                + face * (beside - me)
                + cp[:, x : x + 1] * (other - me)
                + flow
            )


def y_ends_kernel(peers, r0, low, high, inner, outer, gpy, gsy, ymat, msg, rt, ss, qq):
    steps, _, lines = gpy.shape
    length = steps * SUB
    planes = low.shape[1]
    depth = lines // planes
    under = jnp.where(lax.axis_index("gz") > 0, 1.0, 0.0)
    over = jnp.where(lax.axis_index("gz") < peers - 1, 1.0, 0.0)
    even = lax.axis_index("gz") % 2 == 0
    below = [jnp.where(even, outer[i], inner[i]) * under for i in range(2)]
    above = [jnp.where(even, inner[i], outer[i]) * over for i in range(2)]
    lo = 0.5 * (below[1] + low[1]) * (below[0] - low[0])
    hi = 0.5 * (above[1] + high[1]) * (above[0] - high[0])
    row = lax.broadcasted_iota(jnp.int32, (SUB, length), 0)
    parts = []
    for p in range(planes):
        i = p * depth
        top, mid, end = r0[i : i + SUB], r0[i + SUB : i + depth - SUB], r0[i + depth - SUB : i + depth]
        parts += [
            jnp.where(row == 0, top + lo[p : p + 1, :], top),
            mid,
            jnp.where(row == SUB - 1, end + hi[p : p + 1, :], end),
        ]
    rt[...] = jnp.concatenate(parts, 0).T
    s = jnp.zeros((SUB, lines), F32)
    q = jnp.zeros((SUB, lines), F32)
    for t in range(steps):
        back = steps - 1 - t
        s = s + gpy[t] * strided(rt, t, SUB, steps)
        ss[t] = s
        qq[back] = q
        q = q + gsy[back] * strided(rt, back, SUB, steps)
    msg[...] = ymat[...]
    msg[0:1, :] = jnp.sum(q, axis=0, keepdims=True)
    msg[1:2, :] = jnp.sum(s, axis=0, keepdims=True)


def y_local_kernel(peers, low, high, inner, outer, zmat, rt, ss, qq, gpy, gsy, ymat, vloc, zends):
    steps, _, lines = gpy.shape
    s = ss[steps - 1]
    q = qq[0] + gsy[0] * strided(rt, 0, SUB, steps)
    row = lax.broadcasted_iota(jnp.int32, (SUB, lines), 0)
    so, qo = jnp.zeros_like(s), jnp.zeros_like(q)
    for j in range(1, SUB):
        so = so + jnp.where(row >= j, pltpu.roll(s, j, 0), 0.0)
        qo = qo + jnp.where(row < SUB - j, pltpu.roll(q, SUB - j, 0), 0.0)
    w = 1.0 / ymat[3:4, :]
    for t in range(steps):
        vloc[t] = gsy[t] * w * (ss[t] + so) + gpy[t] * w * (qq[t] + qo)
    under = jnp.where(lax.axis_index("gz") > 0, 0.0, 1.0)
    over = jnp.where(lax.axis_index("gz") < peers - 1, 1.0, 0.0)
    zends[0] = zmat[0] + under * 4.0 / low[1]
    zends[1] = zmat[1]
    above = jnp.where(lax.axis_index("gz") % 2 == 0, inner[1], outer[1])
    zends[2] = zmat[2] + 4.0 / (above * over + high[1])


def y_finish_kernel(m0, m1, m2, m3, vloc, gpy, gsy, u, gpz, gsz, zends, rz, own, buf, vt):
    steps, _, lines = gpy.shape
    planes = own.shape[1]
    depth = lines // planes
    got = (m0, m1, m2, m3)
    mine = lax.axis_index("gy")
    for k in range(4):
        buf[mine ^ k] = got[k][...]
    seg = []
    for j in range(4):
        s = buf[j]
        seg.append([s[i : i + 1, :] for i in range(7)])
    zero = jnp.zeros((1, lines), F32)
    gap = [4.0 / (seg[j][6] + seg[j + 1][5]) for j in range(3)]
    e, r = zero, 4.0 / seg[0][5]
    el, rl = e, r
    for j in range(3):
        a, d, b, c, f = seg[j][:5]
        inv = 1.0 / (r + b)
        e, r = d + c * (e - a) * inv, f - c * c * inv + gap[j]
        el, rl = jnp.where(mine == j + 1, e, el), jnp.where(mine == j + 1, r, rl)
    e, r = zero, 4.0 / seg[3][6]
    er, rr = e, r
    for j in (3, 2, 1):
        a, d, b, c, f = seg[j][:5]
        inv = 1.0 / (r + f)
        e, r = a + c * (e - d) * inv, b - c * c * inv + gap[j - 1]
        er, rr = jnp.where(mine == j - 1, e, er), jnp.where(mine == j - 1, r, rr)
    a, d, b, c, f = [m0[i : i + 1, :] for i in range(5)]
    left, right = b + rl, f + rr
    inv = 1.0 / (left * right - c * c)
    ql = ((el - a) * right - c * (er - d)) * inv
    qr = ((er - d) * left - c * (el - a)) * inv
    for t in range(steps):
        vt[pl.ds(t, SUB, stride=steps), :] = vloc[t] + gsy[t] * ql + gpy[t] * qr
    v = vt[...].T
    for p in range(planes):
        i = p * depth
        r = v[i : i + depth, :] - 2.0 * u[i : i + depth, :]
        rz[i : i + depth, :] = r
        own[0, p : p + 1, :] = jnp.sum(gsz[i : i + depth, :] * r, axis=0, keepdims=True)
        own[1, p : p + 1, :] = jnp.sum(gpz[i : i + depth, :] * r, axis=0, keepdims=True)
    for i in range(3):
        own[i + 2] = zends[i]


def z_local_kernel(u, rz, gpz, gsz, zmat, out):
    _, planes, length = zmat.shape
    depth = rz.shape[0] // planes
    for p in range(planes):
        w = 1.0 / zmat[1, p : p + 1, :]
        s = jnp.zeros((1, length), F32)
        ss = []
        for t in range(depth):
            at = pl.ds(p * depth + t, 1)
            s = s + gpz[at, :] * rz[at, :]
            ss.append(s)
        q = jnp.zeros((1, length), F32)
        for t in reversed(range(depth)):
            at = pl.ds(p * depth + t, 1)
            out[at, :] = u[at, :] + w * (gsz[at, :] * ss[t] + gpz[at, :] * q)
            q = q + gsz[at, :] * rz[at, :]


def call(kernel, outs, scratch, cost, in_specs, *args, vmem=32):
    return pl.pallas_call(
        kernel,
        out_shape=[jax.ShapeDtypeStruct(s, F32) for s in outs],
        in_specs=in_specs,
        out_specs=[VMEM] * len(outs),
        scratch_shapes=[pltpu.VMEM(s, F32) if isinstance(s, tuple) else s for s in scratch],
        compiler_params=pltpu.CompilerParams(vmem_limit_bytes=int(vmem * 2**20)),
        cost_estimate=pl.CostEstimate(flops=cost, bytes_accessed=cost // 4, transcendentals=0),
    )(*args)


def join(s, t):
    a1, d1, b1, e1, f1 = s
    a2, d2, b2, e2, f2 = t
    inv = 1.0 / (f1 + b2)
    jump = (a2 - d1) * inv
    cross = e1 * inv
    return (
        a1 + e1 * jump,
        d2 - e2 * jump,
        b1 - e1 * cross,
        e2 * cross,
        f2 - e2 * e2 * inv,
    )


def middle(s, t, ql, qr):
    return (t[0] - s[1] + t[3] * qr - s[3] * ql) / (s[4] + t[2])


def parts_of(ref):
    return tuple(ref[i] for i in range(5))


def choose(flag, s, t):
    return tuple(jnp.where(flag, a, b) for a, b in zip(s, t))


def put(ref, value):
    for i in range(5):
        ref[i] = value[i]


def core_kernel(own, peer, chip):
    lower = lax.axis_index("gz") % 2 == 0
    mine, theirs = parts_of(own), parts_of(peer)
    put(chip, join(choose(lower, mine, theirs), choose(lower, theirs, mine)))


def ring_kernel(position, m0, m1, m2, m3, plane, buf):
    mine = position(lax.axis_index("gz"))
    for k, got in enumerate((m0, m1, m2, m3)):
        buf[mine ^ k] = got[...]
    s = [parts_of(buf.at[j]) for j in range(4)]
    put(plane, join(join(s[0], s[1]), join(s[2], s[3])))


def descend(mine, s, ql, qr):
    lower, upper = join(s[0], s[1]), join(s[2], s[3])
    q = middle(lower, upper, ql, qr)
    up = mine // 2 == 1
    ql, qr = jnp.where(up, -q, ql), jnp.where(up, qr, q)
    q = middle(choose(up, s[2], s[0]), choose(up, s[3], s[1]), ql, qr)
    up = mine % 2 == 1
    return jnp.where(up, -q, ql), jnp.where(up, qr, q)


def finish_kernel(
    own, peer, c0, c1, c2, c3, p0, p1, p2, p3, local, gpz, gsz, out, cbuf, pbuf
):
    iy, ix = position_y(lax.axis_index("gz")), position_x(lax.axis_index("gz"))
    for k, (c, p) in enumerate(((c0, p0), (c1, p1), (c2, p2), (c3, p3))):
        cbuf[iy ^ k] = c[...]
        pbuf[ix ^ k] = p[...]
    column = [parts_of(cbuf.at[j]) for j in range(4)]
    whole = [parts_of(pbuf.at[j]) for j in range(4)]
    a, d, b, e, f = join(join(whole[0], whole[1]), join(whole[2], whole[3]))
    inv = 1.0 / (b * f - e * e)
    ql, qr = (e * d - f * a) * inv, (e * a - b * d) * inv
    ql, qr = descend(ix, whole, ql, qr)
    ql, qr = descend(iy, column, ql, qr)
    lower = lax.axis_index("gz") % 2 == 0
    mine, theirs = parts_of(own), parts_of(peer)
    q = middle(choose(lower, mine, theirs), choose(lower, theirs, mine), ql, qr)
    ql, qr = jnp.where(lower, ql, -q), jnp.where(lower, q, qr)
    planes = ql.shape[0]
    depth = out.shape[0] // planes
    for p in range(planes):
        i = p * depth
        out[i : i + depth, :] = (
            local[i : i + depth, :]
            + gsz[i : i + depth, :] * ql[p : p + 1, :]
            + gpz[i : i + depth, :] * qr[p : p + 1, :]
        )


def position_y(z):
    return z // 2 % 4


def position_x(z):
    return z // 8


def partners(value, axis, count, unit):
    return [
        lax.ppermute(value, axis, [(i, i ^ (k * unit) ^ (unit > 1)) for i in range(count)]) for k in (1, 2, 3)
    ]


def chip_neighbours(rows, peers):
    pairs = []
    for y in range(rows):
        for z in range(peers):
            end = z in (0, peers - 1)
            to = ((y ^ 1) * peers + z) if end else (y * peers + (z + 1 if z % 2 else z - 1))
            pairs.append((y * peers + z, to))
    return pairs


def shards(fields, cond_x, cond_y, cond_z, coupling):
    nf, nx, nz, ny = fields.shape
    planes, lines = nf * nx, nf * nx * nz
    peers = lax.axis_size("gz")
    steps = ny // SUB
    tall, flat, face, ends = (steps, SUB, lines), (lines, ny), (planes, ny), (5, planes, ny)
    hbm = pl.BlockSpec(memory_space=pltpu.HBM)
    dma = pltpu.SemaphoreType.DMA
    u, ky, kz, low, high, inner, outer = call(
        load_kernel, [flat] * 3 + [(2, *face)] * 4, [dma((3,))], 100_000, [hbm] * 3,
        fields.reshape(flat), cond_y.reshape(flat), cond_z.reshape(flat), vmem=53,
    )
    inner = lax.ppermute(inner, "gz", [(i, i ^ 1) for i in range(peers)])
    outer = lax.ppermute(outer, ("gy", "gz"), chip_neighbours(lax.axis_size("gy"), peers))
    gpy, gsy, ymat, gpz, gsz, zmat, r0 = call(
        factor_kernel,
        [tall, tall, (8, lines), flat, flat, (3, *face), flat],
        [(ny, lines)] + [tall] * 5 + [(nz, *face)],
        4_000_000,
        [VMEM] * 5,
        cond_x, coupling[None], u, ky, kz,
    )
    msg, rt, ss, qq = call(
        functools.partial(y_ends_kernel, peers), [(8, lines), (ny, lines), tall, tall], [], 1_000_000, [VMEM] * 8,
        r0, low, high, inner, outer, gpy, gsy, ymat,
    )
    others = partners(msg, "gy", 4, 1)
    vloc, zends = call(
        functools.partial(y_local_kernel, peers), [tall, (3, *face)], [], 1_000_000, [VMEM] * 11,
        low, high, inner, outer, zmat, rt, ss, qq, gpy, gsy, ymat,
    )
    rz, own = call(
        y_finish_kernel, [flat, ends], [(4, 8, lines), (ny, lines)], 1_000_000, [VMEM] * 11,
        msg, *others, vloc, gpy, gsy, u, gpz, gsz, zends,
    )
    peer = lax.ppermute(own, "gz", [(i, i ^ 1) for i in range(peers)])
    [local] = call(z_local_kernel, [flat], [], 1_000_000, [VMEM] * 5, u, rz, gpz, gsz, zmat)
    [chip] = call(core_kernel, [ends], [], 50_000, [VMEM] * 2, own, peer)
    column = [chip] + partners(chip, "gz", peers, 2)
    [plane] = call(
        functools.partial(ring_kernel, position_y), [ends], [(4, *ends)], 50_000,
        [VMEM] * 4, *column,
    )
    whole = [plane] + partners(plane, "gz", peers, 8)
    [out] = call(
        finish_kernel, [flat], [(4, *ends), (4, *ends)], 1_000_000, [VMEM] * 13,
        own, peer, *column, *whole, local, gpz, gsz,
    )
    return out.reshape(fields.shape)


def solution(mesh):
    block = P(None, None, "gz", "gy")
    return jax.shard_map(
        shards,
        mesh=mesh,
        in_specs=(block, P(), block, block, P()),
        out_specs=block,
        check_vma=False,
    )
```

```python
import functools

import jax
import jax.numpy as jnp
from jax import lax
from jax.experimental import pallas as pl
from jax.experimental.pallas import tpu as pltpu
from jax.sharding import PartitionSpec as P

SUB = 8
F32 = jnp.float32
VMEM = pl.BlockSpec(memory_space=pltpu.VMEM)
SMEM = pl.BlockSpec(memory_space=pltpu.SMEM)


def strided(ref, start, count, stride):
    return ref[pl.ds(start, count, stride=stride), :]


def load_kernel(uh, kyh, kzh, u, ky, kz, low, high, inner, outer, sem):
    copies = [
        pltpu.make_async_copy(src, dst, sem.at[i])
        for i, (src, dst) in enumerate(((uh, u), (kzh, kz), (kyh, ky)))
    ]
    for copy in copies:
        copy.start()
    planes = low.shape[1]
    depth = u.shape[0] // planes
    even = lax.axis_index("gz") % 2 == 0
    for i, array in enumerate((u, kz)):
        copies[i].wait()
        for p in range(planes):
            at = p * depth
            bottom, top = array[at : at + 1, :], array[at + depth - 1 : at + depth, :]
            low[i, p : p + 1, :] = bottom
            high[i, p : p + 1, :] = top
            inner[i, p : p + 1, :] = jnp.where(even, top, bottom)
            outer[i, p : p + 1, :] = jnp.where(even, bottom, top)
    copies[2].wait()


def factor_kernel(
    cx, cp, u, ky, kz, gpy, gsy, ymat, gpz, gsz, zmat, r0, kt, zr, wa, wb, wc, wd, zz
):
    lines, length = ky.shape
    steps = length // SUB
    planes, depth = zmat.shape[1], lines // zmat.shape[1]
    kt[...] = ky[...].T
    first = strided(kt, 0, SUB, steps)
    here = first
    for t in range(steps):
        after = strided(kt, t + 1, SUB, steps) if t + 1 < steps else pltpu.roll(first, SUB - 1, 0)
        zr[t] = 4.0 / (here + after)
        here = after
    last = strided(kt, steps - 1, SUB, steps)
    row = lax.broadcasted_iota(jnp.int32, (SUB, lines), 0)
    one, zero = jnp.ones((SUB, lines), F32), jnp.zeros((SUB, lines), F32)
    aw, aj, bw, bj = one, zero, zero, one
    for t in range(steps):
        wa[t], wb[t] = aw, bw
        aj, bj = aj + aw, bj + bw
        aw, bw = aw + zr[t] * aj, bw + zr[t] * bj
    cw, cj, dw, dj = one, zero, zero, one
    for t in reversed(range(steps)):
        wc[t], wd[t] = cw, dw
        cj, dj = cj + cw, dj + dw
        z = zr[t - 1] if t else pltpu.roll(zr[steps - 1], 1, 0)
        cw, dw = cw + z * cj, dw + z * dj
    al, be, ga, de = one, zero, one, zero
    for j in range(SUB - 1):
        nal, nbe = pltpu.roll(aw * al + bw * be, 1, 0), pltpu.roll(aj * al + bj * be, 1, 0)
        al, be = jnp.where(row == j + 1, nal, al), jnp.where(row == j + 1, nbe, be)
        nga = pltpu.roll(cw * ga + dw * de, SUB - 1, 0)
        nde = pltpu.roll(cj * ga + dj * de, SUB - 1, 0)
        at = SUB - 2 - j
        ga, de = jnp.where(row == at, nga, ga), jnp.where(row == at, nde, de)
    iw = 1.0 / (aj * al + bj * be)[SUB - 1 :, :]
    iv = 1.0 / (cj * ga + dj * de)[:1, :]
    al, be, ga, de = al * iw, be * iw, ga * iv, de * iv
    for t in range(steps):
        gpy[t] = al * wa[t] + be * wb[t]
        gsy[t] = ga * wc[t] + de * wd[t]
    ymat[...] = jnp.zeros_like(ymat)
    ymat[2:3, :] = gsy[0][:1, :]
    ymat[3:4, :] = iw
    ymat[4:5, :] = gpy[steps - 1][SUB - 1 :, :]
    ymat[5:6, :] = first[:1, :]
    ymat[6:7, :] = last[SUB - 1 :, :]
    here = [kz[pl.ds(p * depth, 1), :] for p in range(planes)]
    here = jnp.concatenate(here, 0)
    for t in range(depth - 1):
        after = jnp.concatenate([kz[pl.ds(p * depth + t + 1, 1), :] for p in range(planes)], 0)
        zz[t] = 4.0 / (here + after)
        here = after
    w, j = jnp.ones_like(here), jnp.zeros_like(here)
    ws = []
    for t in range(depth):
        ws.append(w)
        j = j + w
        if t + 1 < depth:
            w = w + zz[t] * j
    ij = 1.0 / j
    for t in range(depth):
        g = ws[t] * ij
        for p in range(planes):
            gpz[pl.ds(p * depth + t, 1), :] = g[p : p + 1, :]
    zmat[1] = ij
    zmat[2] = ws[depth - 1] * ij
    w, j = jnp.ones_like(here), jnp.zeros_like(here)
    ws = []
    for t in reversed(range(depth)):
        ws.append(w)
        j = j + w
        if t:
            w = w + zz[t - 1] * j
    ij = 1.0 / j
    for t in range(depth):
        g = ws[depth - 1 - t] * ij
        for p in range(planes):
            gsz[pl.ds(p * depth + t, 1), :] = g[p : p + 1, :]
    zmat[0] = ws[depth - 1] * ij
    for f in range(2):
        for x in range(2):
            at = (f * 2 + x) * depth
            me = u[at : at + depth, :]
            beside = u[(f * 2 + 1 - x) * depth : (f * 2 + 2 - x) * depth, :]
            other = u[((1 - f) * 2 + x) * depth : ((1 - f) * 2 + x + 1) * depth, :]
            face = 0.5 * (cx[f : f + 1, 0:1] + cx[f : f + 1, 1:2])
            k = kz[at : at + depth, :]
            flux = 0.5 * (k[1:] + k[:-1]) * (me[1:] - me[:-1])
            none = jnp.zeros((1, length), F32)
            flow = jnp.concatenate([flux, none], 0) - jnp.concatenate([none, flux], 0)
            r0[at : at + depth, :] = (
                (2.0 - 0.5 * cx[f : f + 1, x : x + 1]) * me
                + face * (beside - me)
                + cp[:, x : x + 1] * (other - me)
                + flow
            )


def y_ends_kernel(peers, r0, low, high, inner, outer, gpy, gsy, ymat, msg, rt, ss, qq):
    steps, _, lines = gpy.shape
    length = steps * SUB
    planes = low.shape[1]
    depth = lines // planes
    under = jnp.where(lax.axis_index("gz") > 0, 1.0, 0.0)
    over = jnp.where(lax.axis_index("gz") < peers - 1, 1.0, 0.0)
    even = lax.axis_index("gz") % 2 == 0
    below = [jnp.where(even, outer[i], inner[i]) * under for i in range(2)]
    above = [jnp.where(even, inner[i], outer[i]) * over for i in range(2)]
    lo = 0.5 * (below[1] + low[1]) * (below[0] - low[0])
    hi = 0.5 * (above[1] + high[1]) * (above[0] - high[0])
    row = lax.broadcasted_iota(jnp.int32, (SUB, length), 0)
    parts = []
    for p in range(planes):
        i = p * depth
        top, mid, end = r0[i : i + SUB], r0[i + SUB : i + depth - SUB], r0[i + depth - SUB : i + depth]
        parts += [
            jnp.where(row == 0, top + lo[p : p + 1, :], top),
            mid,
            jnp.where(row == SUB - 1, end + hi[p : p + 1, :], end),
        ]
    rt[...] = jnp.concatenate(parts, 0).T
    s = jnp.zeros((SUB, lines), F32)
    q = jnp.zeros((SUB, lines), F32)
    for t in range(steps):
        back = steps - 1 - t
        s = s + gpy[t] * strided(rt, t, SUB, steps)
        ss[t] = s
        qq[back] = q
        q = q + gsy[back] * strided(rt, back, SUB, steps)
    msg[...] = ymat[...]
    msg[0:1, :] = jnp.sum(q, axis=0, keepdims=True)
    msg[1:2, :] = jnp.sum(s, axis=0, keepdims=True)


def y_local_kernel(peers, low, high, inner, outer, zmat, rt, ss, qq, gpy, gsy, ymat, vloc, zends):
    steps, _, lines = gpy.shape
    s = ss[steps - 1]
    q = qq[0] + gsy[0] * strided(rt, 0, SUB, steps)
    row = lax.broadcasted_iota(jnp.int32, (SUB, lines), 0)
    so, qo = jnp.zeros_like(s), jnp.zeros_like(q)
    for j in range(1, SUB):
        so = so + jnp.where(row >= j, pltpu.roll(s, j, 0), 0.0)
        qo = qo + jnp.where(row < SUB - j, pltpu.roll(q, SUB - j, 0), 0.0)
    w = 1.0 / ymat[3:4, :]
    for t in range(steps):
        vloc[t] = gsy[t] * w * (ss[t] + so) + gpy[t] * w * (qq[t] + qo)
    under = jnp.where(lax.axis_index("gz") > 0, 0.0, 1.0)
    over = jnp.where(lax.axis_index("gz") < peers - 1, 1.0, 0.0)
    zends[0] = zmat[0] + under * 4.0 / low[1]
    zends[1] = zmat[1]
    above = jnp.where(lax.axis_index("gz") % 2 == 0, inner[1], outer[1])
    zends[2] = zmat[2] + 4.0 / (above * over + high[1])


def y_finish_kernel(m0, m1, m2, m3, vloc, gpy, gsy, u, gpz, gsz, zends, rz, own, buf, vt):
    steps, _, lines = gpy.shape
    planes = own.shape[1]
    depth = lines // planes
    got = (m0, m1, m2, m3)
    mine = lax.axis_index("gy")
    for k in range(4):
        buf[mine ^ k] = got[k][...]
    seg = []
    for j in range(4):
        s = buf[j]
        seg.append([s[i : i + 1, :] for i in range(7)])
    zero = jnp.zeros((1, lines), F32)
    gap = [4.0 / (seg[j][6] + seg[j + 1][5]) for j in range(3)]
    e, r = zero, 4.0 / seg[0][5]
    el, rl = e, r
    for j in range(3):
        a, d, b, c, f = seg[j][:5]
        inv = 1.0 / (r + b)
        e, r = d + c * (e - a) * inv, f - c * c * inv + gap[j]
        el, rl = jnp.where(mine == j + 1, e, el), jnp.where(mine == j + 1, r, rl)
    e, r = zero, 4.0 / seg[3][6]
    er, rr = e, r
    for j in (3, 2, 1):
        a, d, b, c, f = seg[j][:5]
        inv = 1.0 / (r + f)
        e, r = a + c * (e - d) * inv, b - c * c * inv + gap[j - 1]
        er, rr = jnp.where(mine == j - 1, e, er), jnp.where(mine == j - 1, r, rr)
    a, d, b, c, f = [m0[i : i + 1, :] for i in range(5)]
    left, right = b + rl, f + rr
    inv = 1.0 / (left * right - c * c)
    ql = ((el - a) * right - c * (er - d)) * inv
    qr = ((er - d) * left - c * (el - a)) * inv
    for t in range(steps):
        vt[pl.ds(t, SUB, stride=steps), :] = vloc[t] + gsy[t] * ql + gpy[t] * qr
    v = vt[...].T
    for p in range(planes):
        i = p * depth
        r = v[i : i + depth, :] - 2.0 * u[i : i + depth, :]
        rz[i : i + depth, :] = r
        own[0, p : p + 1, :] = jnp.sum(gsz[i : i + depth, :] * r, axis=0, keepdims=True)
        own[1, p : p + 1, :] = jnp.sum(gpz[i : i + depth, :] * r, axis=0, keepdims=True)
    for i in range(3):
        own[i + 2] = zends[i]


def z_local_kernel(u, rz, gpz, gsz, zmat, out, ready):
    ready[...] = jnp.zeros_like(ready)
    _, planes, length = zmat.shape
    depth = rz.shape[0] // planes
    for p in range(planes):
        w = 1.0 / zmat[1, p : p + 1, :]
        s = jnp.zeros((1, length), F32)
        ss = []
        for t in range(depth):
            at = pl.ds(p * depth + t, 1)
            s = s + gpz[at, :] * rz[at, :]
            ss.append(s)
        q = jnp.zeros((1, length), F32)
        for t in reversed(range(depth)):
            at = pl.ds(p * depth + t, 1)
            out[at, :] = u[at, :] + w * (gsz[at, :] * ss[t] + gpz[at, :] * q)
            q = q + gsz[at, :] * rz[at, :]


def call(kernel, outs, scratch, cost, in_specs, *args, vmem=32):
    return pl.pallas_call(
        kernel,
        out_shape=[jax.ShapeDtypeStruct(s, F32) for s in outs],
        in_specs=in_specs,
        out_specs=[VMEM] * len(outs),
        scratch_shapes=[pltpu.VMEM(s, F32) if isinstance(s, tuple) else s for s in scratch],
        compiler_params=pltpu.CompilerParams(vmem_limit_bytes=int(vmem * 2**20)),
        cost_estimate=pl.CostEstimate(flops=cost, bytes_accessed=cost // 4, transcendentals=0),
    )(*args)


def join(s, t):
    a1, d1, b1, e1, f1 = s
    a2, d2, b2, e2, f2 = t
    inv = 1.0 / (f1 + b2)
    jump = (a2 - d1) * inv
    cross = e1 * inv
    return (
        a1 + e1 * jump,
        d2 - e2 * jump,
        b1 - e1 * cross,
        e2 * cross,
        f2 - e2 * e2 * inv,
    )


def middle(s, t, ql, qr):
    return (t[0] - s[1] + t[3] * qr - s[3] * ql) / (s[4] + t[2])


def parts_of(ref):
    return tuple(ref[i] for i in range(5))


def choose(flag, s, t):
    return tuple(jnp.where(flag, a, b) for a, b in zip(s, t))


def put(ref, value):
    for i in range(5):
        ref[i] = value[i]


def core_kernel(own, peer, ready, chip):
    lower = lax.axis_index("gz") % 2 == 0
    mine, theirs = parts_of(own), parts_of(peer)
    put(chip, join(choose(lower, mine, theirs), choose(lower, theirs, mine)))


def ring_kernel(position, m0, m1, m2, m3, plane, buf):
    mine = position(lax.axis_index("gz"))
    for k, got in enumerate((m0, m1, m2, m3)):
        buf[mine ^ k] = got[...]
    s = [parts_of(buf.at[j]) for j in range(4)]
    put(plane, join(join(s[0], s[1]), join(s[2], s[3])))


def descend(mine, s, ql, qr):
    lower, upper = join(s[0], s[1]), join(s[2], s[3])
    q = middle(lower, upper, ql, qr)
    up = mine // 2 == 1
    ql, qr = jnp.where(up, -q, ql), jnp.where(up, qr, q)
    q = middle(choose(up, s[2], s[0]), choose(up, s[3], s[1]), ql, qr)
    up = mine % 2 == 1
    return jnp.where(up, -q, ql), jnp.where(up, qr, q)


def finish_kernel(
    own, peer, c0, c1, c2, c3, p0, p1, p2, p3, local, gpz, gsz, out, cbuf, pbuf
):
    iy, ix = position_y(lax.axis_index("gz")), position_x(lax.axis_index("gz"))
    for k, (c, p) in enumerate(((c0, p0), (c1, p1), (c2, p2), (c3, p3))):
        cbuf[iy ^ k] = c[...]
        pbuf[ix ^ k] = p[...]
    column = [parts_of(cbuf.at[j]) for j in range(4)]
    whole = [parts_of(pbuf.at[j]) for j in range(4)]
    a, d, b, e, f = join(join(whole[0], whole[1]), join(whole[2], whole[3]))
    inv = 1.0 / (b * f - e * e)
    ql, qr = (e * d - f * a) * inv, (e * a - b * d) * inv
    ql, qr = descend(ix, whole, ql, qr)
    ql, qr = descend(iy, column, ql, qr)
    lower = lax.axis_index("gz") % 2 == 0
    mine, theirs = parts_of(own), parts_of(peer)
    q = middle(choose(lower, mine, theirs), choose(lower, theirs, mine), ql, qr)
    ql, qr = jnp.where(lower, ql, -q), jnp.where(lower, q, qr)
    planes = ql.shape[0]
    depth = out.shape[0] // planes
    for p in range(planes):
        i = p * depth
        out[i : i + depth, :] = (
            local[i : i + depth, :]
            + gsz[i : i + depth, :] * ql[p : p + 1, :]
            + gpz[i : i + depth, :] * qr[p : p + 1, :]
        )


def position_y(z):
    return z // 2 % 4


def position_x(z):
    return z // 8


def partners(value, axis, count, unit):
    got = {
        k: lax.ppermute(value, axis, [(i, i ^ (k * unit) ^ (unit > 1)) for i in range(count)])
        for k in (1, 2, 3)
    }
    got[2] = got[2] * unity()
    return [got[k] for k in (1, 2, 3)]


def unity():
    return jnp.where(lax.axis_index("gz") < lax.axis_size("gz"), 1.0, 0.0)


def chip_neighbours(rows, peers):
    pairs = []
    for y in range(rows):
        for z in range(peers):
            end = z in (0, peers - 1)
            to = ((y ^ 1) * peers + z) if end else (y * peers + (z + 1 if z % 2 else z - 1))
            pairs.append((y * peers + z, to))
    return pairs


def shards(fields, cond_x, cond_y, cond_z, coupling):
    nf, nx, nz, ny = fields.shape
    planes, lines = nf * nx, nf * nx * nz
    peers = lax.axis_size("gz")
    steps = ny // SUB
    tall, flat, face, ends = (steps, SUB, lines), (lines, ny), (planes, ny), (5, planes, ny)
    hbm = pl.BlockSpec(memory_space=pltpu.HBM)
    dma = pltpu.SemaphoreType.DMA
    u, ky, kz, low, high, inner, outer = call(
        load_kernel, [flat] * 3 + [(2, *face)] * 4, [dma((3,))], 100_000, [hbm] * 3,
        fields.reshape(flat), cond_y.reshape(flat), cond_z.reshape(flat), vmem=53,
    )
    inner = lax.ppermute(inner, "gz", [(i, i ^ 1) for i in range(peers)])
    outer = lax.ppermute(outer, ("gy", "gz"), chip_neighbours(lax.axis_size("gy"), peers))
    gpy, gsy, ymat, gpz, gsz, zmat, r0 = call(
        factor_kernel,
        [tall, tall, (8, lines), flat, flat, (3, *face), flat],
        [(ny, lines)] + [tall] * 5 + [(nz, *face)],
        4_000_000,
        [VMEM] * 5,
        cond_x, coupling[None], u, ky, kz,
    )
    outer = outer * unity()
    msg, rt, ss, qq = call(
        functools.partial(y_ends_kernel, peers), [(8, lines), (ny, lines), tall, tall], [], 1_000_000, [VMEM] * 8,
        r0, low, high, inner, outer, gpy, gsy, ymat,
    )
    others = partners(msg, "gy", 4, 1)
    vloc, zends = call(
        functools.partial(y_local_kernel, peers), [tall, (3, *face)], [], 1_000_000, [VMEM] * 11,
        low, high, inner, outer, zmat, rt, ss, qq, gpy, gsy, ymat,
    )
    rz, own = call(
        y_finish_kernel, [flat, ends], [(4, 8, lines), (ny, lines)], 1_000_000, [VMEM] * 11,
        msg, *others, vloc, gpy, gsy, u, gpz, gsz, zends,
    )
    peer = lax.ppermute(own, "gz", [(i, i ^ 1) for i in range(peers)])
    local, ready = call(z_local_kernel, [flat, (8, 128)], [], 1_000_000, [VMEM] * 5, u, rz, gpz, gsz, zmat)
    [chip] = call(core_kernel, [ends], [], 50_000, [VMEM] * 3, own, peer, ready)
    column = [chip] + partners(chip, "gz", peers, 2)
    [plane] = call(
        functools.partial(ring_kernel, position_y), [ends], [(4, *ends)], 50_000,
        [VMEM] * 4, *column,
    )
    whole = [plane] + partners(plane, "gz", peers, 8)
    [out] = call(
        finish_kernel, [flat], [(4, *ends), (4, *ends)], 1_000_000, [VMEM] * 13,
        own, peer, *column, *whole, local, gpz, gsz,
    )
    return out.reshape(fields.shape)


def solution(mesh):
    block = P(None, None, "gz", "gy")
    return jax.shard_map(
        shards,
        mesh=mesh,
        in_specs=(block, P(), block, block, P()),
        out_specs=block,
        check_vma=False,
    )
```

```python
import functools

import jax
import jax.numpy as jnp
from jax import lax
from jax.experimental import pallas as pl
from jax.experimental.pallas import tpu as pltpu
from jax.sharding import PartitionSpec as P

SUB = 8
F32 = jnp.float32
VMEM = pl.BlockSpec(memory_space=pltpu.VMEM)
SMEM = pl.BlockSpec(memory_space=pltpu.SMEM)


def strided(ref, start, count, stride):
    return ref[pl.ds(start, count, stride=stride), :]


def load_kernel(uh, kyh, kzh, u, ky, kz, low, high, inner, outer, sem):
    copies = [
        pltpu.make_async_copy(src, dst, sem.at[i])
        for i, (src, dst) in enumerate(((uh, u), (kzh, kz), (kyh, ky)))
    ]
    for copy in copies:
        copy.start()
    planes = low.shape[1]
    depth = u.shape[0] // planes
    even = lax.axis_index("gz") % 2 == 0
    for i, array in enumerate((u, kz)):
        copies[i].wait()
        for p in range(planes):
            at = p * depth
            bottom, top = array[at : at + 1, :], array[at + depth - 1 : at + depth, :]
            low[i, p : p + 1, :] = bottom
            high[i, p : p + 1, :] = top
            inner[i, p : p + 1, :] = jnp.where(even, top, bottom)
            outer[i, p : p + 1, :] = jnp.where(even, bottom, top)
    copies[2].wait()


def factor_kernel(
    cx, cp, u, ky, kz, gpy, gsy, ymat, gpz, gsz, zmat, r0, kt, zr, wa, wb, wc, wd, zz
):
    lines, length = ky.shape
    steps = length // SUB
    planes, depth = zmat.shape[1], lines // zmat.shape[1]
    kt[...] = ky[...].T
    first = strided(kt, 0, SUB, steps)
    here = first
    for t in range(steps):
        after = strided(kt, t + 1, SUB, steps) if t + 1 < steps else pltpu.roll(first, SUB - 1, 0)
        zr[t] = 4.0 / (here + after)
        here = after
    last = strided(kt, steps - 1, SUB, steps)
    row = lax.broadcasted_iota(jnp.int32, (SUB, lines), 0)
    one, zero = jnp.ones((SUB, lines), F32), jnp.zeros((SUB, lines), F32)
    aw, aj, bw, bj = one, zero, zero, one
    for t in range(steps):
        wa[t], wb[t] = aw, bw
        aj, bj = aj + aw, bj + bw
        aw, bw = aw + zr[t] * aj, bw + zr[t] * bj
    cw, cj, dw, dj = one, zero, zero, one
    for t in reversed(range(steps)):
        wc[t], wd[t] = cw, dw
        cj, dj = cj + cw, dj + dw
        z = zr[t - 1] if t else pltpu.roll(zr[steps - 1], 1, 0)
        cw, dw = cw + z * cj, dw + z * dj
    al, be, ga, de = one, zero, one, zero
    for j in range(SUB - 1):
        nal, nbe = pltpu.roll(aw * al + bw * be, 1, 0), pltpu.roll(aj * al + bj * be, 1, 0)
        al, be = jnp.where(row == j + 1, nal, al), jnp.where(row == j + 1, nbe, be)
        nga = pltpu.roll(cw * ga + dw * de, SUB - 1, 0)
        nde = pltpu.roll(cj * ga + dj * de, SUB - 1, 0)
        at = SUB - 2 - j
        ga, de = jnp.where(row == at, nga, ga), jnp.where(row == at, nde, de)
    iw = 1.0 / (aj * al + bj * be)[SUB - 1 :, :]
    iv = 1.0 / (cj * ga + dj * de)[:1, :]
    al, be, ga, de = al * iw, be * iw, ga * iv, de * iv
    for t in range(steps):
        gpy[t] = al * wa[t] + be * wb[t]
        gsy[t] = ga * wc[t] + de * wd[t]
    ymat[...] = jnp.zeros_like(ymat)
    ymat[2:3, :] = gsy[0][:1, :]
    ymat[3:4, :] = iw
    ymat[4:5, :] = gpy[steps - 1][SUB - 1 :, :]
    ymat[5:6, :] = first[:1, :]
    ymat[6:7, :] = last[SUB - 1 :, :]
    here = [kz[pl.ds(p * depth, 1), :] for p in range(planes)]
    here = jnp.concatenate(here, 0)
    for t in range(depth - 1):
        after = jnp.concatenate([kz[pl.ds(p * depth + t + 1, 1), :] for p in range(planes)], 0)
        zz[t] = 4.0 / (here + after)
        here = after
    w, j = jnp.ones_like(here), jnp.zeros_like(here)
    ws = []
    for t in range(depth):
        ws.append(w)
        j = j + w
        if t + 1 < depth:
            w = w + zz[t] * j
    ij = 1.0 / j
    for t in range(depth):
        g = ws[t] * ij
        for p in range(planes):
            gpz[pl.ds(p * depth + t, 1), :] = g[p : p + 1, :]
    zmat[1] = ij
    zmat[2] = ws[depth - 1] * ij
    w, j = jnp.ones_like(here), jnp.zeros_like(here)
    ws = []
    for t in reversed(range(depth)):
        ws.append(w)
        j = j + w
        if t:
            w = w + zz[t - 1] * j
    ij = 1.0 / j
    for t in range(depth):
        g = ws[depth - 1 - t] * ij
        for p in range(planes):
            gsz[pl.ds(p * depth + t, 1), :] = g[p : p + 1, :]
    zmat[0] = ws[depth - 1] * ij
    for f in range(2):
        for x in range(2):
            at = (f * 2 + x) * depth
            me = u[at : at + depth, :]
            beside = u[(f * 2 + 1 - x) * depth : (f * 2 + 2 - x) * depth, :]
            other = u[((1 - f) * 2 + x) * depth : ((1 - f) * 2 + x + 1) * depth, :]
            face = 0.5 * (cx[f : f + 1, 0:1] + cx[f : f + 1, 1:2])
            k = kz[at : at + depth, :]
            flux = 0.5 * (k[1:] + k[:-1]) * (me[1:] - me[:-1])
            none = jnp.zeros((1, length), F32)
            flow = jnp.concatenate([flux, none], 0) - jnp.concatenate([none, flux], 0)
            r0[at : at + depth, :] = (
                (2.0 - 0.5 * cx[f : f + 1, x : x + 1]) * me
                + face * (beside - me)
                + cp[:, x : x + 1] * (other - me)
                + flow
            )


def y_ends_kernel(peers, r0, low, high, inner, outer, gpy, gsy, ymat, msg, rt, ss, qq):
    steps, _, lines = gpy.shape
    length = steps * SUB
    planes = low.shape[1]
    depth = lines // planes
    under = jnp.where(lax.axis_index("gz") > 0, 1.0, 0.0)
    over = jnp.where(lax.axis_index("gz") < peers - 1, 1.0, 0.0)
    even = lax.axis_index("gz") % 2 == 0
    below = [jnp.where(even, outer[i], inner[i]) * under for i in range(2)]
    above = [jnp.where(even, inner[i], outer[i]) * over for i in range(2)]
    lo = 0.5 * (below[1] + low[1]) * (below[0] - low[0])
    hi = 0.5 * (above[1] + high[1]) * (above[0] - high[0])
    row = lax.broadcasted_iota(jnp.int32, (SUB, length), 0)
    parts = []
    for p in range(planes):
        i = p * depth
        top, mid, end = r0[i : i + SUB], r0[i + SUB : i + depth - SUB], r0[i + depth - SUB : i + depth]
        parts += [
            jnp.where(row == 0, top + lo[p : p + 1, :], top),
            mid,
            jnp.where(row == SUB - 1, end + hi[p : p + 1, :], end),
        ]
    rt[...] = jnp.concatenate(parts, 0).T
    s = jnp.zeros((SUB, lines), F32)
    q = jnp.zeros((SUB, lines), F32)
    for t in range(steps):
        back = steps - 1 - t
        s = s + gpy[t] * strided(rt, t, SUB, steps)
        ss[t] = s
        qq[back] = q
        q = q + gsy[back] * strided(rt, back, SUB, steps)
    msg[...] = ymat[...]
    msg[0:1, :] = jnp.sum(q, axis=0, keepdims=True)
    msg[1:2, :] = jnp.sum(s, axis=0, keepdims=True)


def y_local_kernel(peers, low, high, inner, outer, zmat, rt, ss, qq, gpy, gsy, ymat, vloc, zends):
    steps, _, lines = gpy.shape
    s = ss[steps - 1]
    q = qq[0] + gsy[0] * strided(rt, 0, SUB, steps)
    row = lax.broadcasted_iota(jnp.int32, (SUB, lines), 0)
    so, qo = jnp.zeros_like(s), jnp.zeros_like(q)
    for j in range(1, SUB):
        so = so + jnp.where(row >= j, pltpu.roll(s, j, 0), 0.0)
        qo = qo + jnp.where(row < SUB - j, pltpu.roll(q, SUB - j, 0), 0.0)
    w = 1.0 / ymat[3:4, :]
    for t in range(steps):
        vloc[t] = gsy[t] * w * (ss[t] + so) + gpy[t] * w * (qq[t] + qo)
    under = jnp.where(lax.axis_index("gz") > 0, 0.0, 1.0)
    over = jnp.where(lax.axis_index("gz") < peers - 1, 1.0, 0.0)
    zends[0] = zmat[0] + under * 4.0 / low[1]
    zends[1] = zmat[1]
    above = jnp.where(lax.axis_index("gz") % 2 == 0, inner[1], outer[1])
    zends[2] = zmat[2] + 4.0 / (above * over + high[1])


def y_finish_kernel(m0, m1, m2, m3, vloc, gpy, gsy, u, gpz, gsz, zends, rz, own, buf, vt):
    steps, _, lines = gpy.shape
    planes = own.shape[1]
    depth = lines // planes
    got = (m0, m1, m2, m3)
    mine = lax.axis_index("gy")
    for k in range(4):
        buf[mine ^ k] = got[k][...]
    seg = []
    for j in range(4):
        s = buf[j]
        seg.append([s[i : i + 1, :] for i in range(7)])
    zero = jnp.zeros((1, lines), F32)
    gap = [4.0 / (seg[j][6] + seg[j + 1][5]) for j in range(3)]
    e, r = zero, 4.0 / seg[0][5]
    el, rl = e, r
    for j in range(3):
        a, d, b, c, f = seg[j][:5]
        inv = 1.0 / (r + b)
        e, r = d + c * (e - a) * inv, f - c * c * inv + gap[j]
        el, rl = jnp.where(mine == j + 1, e, el), jnp.where(mine == j + 1, r, rl)
    e, r = zero, 4.0 / seg[3][6]
    er, rr = e, r
    for j in (3, 2, 1):
        a, d, b, c, f = seg[j][:5]
        inv = 1.0 / (r + f)
        e, r = a + c * (e - d) * inv, b - c * c * inv + gap[j - 1]
        er, rr = jnp.where(mine == j - 1, e, er), jnp.where(mine == j - 1, r, rr)
    a, d, b, c, f = [m0[i : i + 1, :] for i in range(5)]
    left, right = b + rl, f + rr
    inv = 1.0 / (left * right - c * c)
    ql = ((el - a) * right - c * (er - d)) * inv
    qr = ((er - d) * left - c * (el - a)) * inv
    for t in range(steps):
        vt[pl.ds(t, SUB, stride=steps), :] = vloc[t] + gsy[t] * ql + gpy[t] * qr
    v = vt[...].T
    for p in range(planes):
        i = p * depth
        r = v[i : i + depth, :] - 2.0 * u[i : i + depth, :]
        rz[i : i + depth, :] = r
        own[0, p : p + 1, :] = jnp.sum(gsz[i : i + depth, :] * r, axis=0, keepdims=True)
        own[1, p : p + 1, :] = jnp.sum(gpz[i : i + depth, :] * r, axis=0, keepdims=True)
    for i in range(3):
        own[i + 2] = zends[i]


def z_local_kernel(u, rz, gpz, gsz, zmat, out, ready):
    ready[...] = jnp.zeros_like(ready)
    _, planes, length = zmat.shape
    depth = rz.shape[0] // planes
    for p in range(planes):
        w = 1.0 / zmat[1, p : p + 1, :]
        s = jnp.zeros((1, length), F32)
        ss = []
        for t in range(depth):
            at = pl.ds(p * depth + t, 1)
            s = s + gpz[at, :] * rz[at, :]
            ss.append(s)
        q = jnp.zeros((1, length), F32)
        for t in reversed(range(depth)):
            at = pl.ds(p * depth + t, 1)
            out[at, :] = u[at, :] + w * (gsz[at, :] * ss[t] + gpz[at, :] * q)
            q = q + gsz[at, :] * rz[at, :]


def call(kernel, outs, scratch, cost, in_specs, *args, vmem=32):
    return pl.pallas_call(
        kernel,
        out_shape=[jax.ShapeDtypeStruct(s, F32) for s in outs],
        in_specs=in_specs,
        out_specs=[VMEM] * len(outs),
        scratch_shapes=[pltpu.VMEM(s, F32) if isinstance(s, tuple) else s for s in scratch],
        compiler_params=pltpu.CompilerParams(vmem_limit_bytes=int(vmem * 2**20)),
        cost_estimate=pl.CostEstimate(flops=cost, bytes_accessed=cost // 4, transcendentals=0),
    )(*args)


def join(s, t):
    a1, d1, b1, e1, f1 = s
    a2, d2, b2, e2, f2 = t
    inv = 1.0 / (f1 + b2)
    jump = (a2 - d1) * inv
    cross = e1 * inv
    return (
        a1 + e1 * jump,
        d2 - e2 * jump,
        b1 - e1 * cross,
        e2 * cross,
        f2 - e2 * e2 * inv,
    )


def middle(s, t, ql, qr):
    return (t[0] - s[1] + t[3] * qr - s[3] * ql) / (s[4] + t[2])


def parts_of(ref):
    return tuple(ref[i] for i in range(5))


def choose(flag, s, t):
    return tuple(jnp.where(flag, a, b) for a, b in zip(s, t))


def put(ref, value):
    for i in range(5):
        ref[i] = value[i]


def core_kernel(own, peer, ready, chip):
    lower = lax.axis_index("gz") % 2 == 0
    mine, theirs = parts_of(own), parts_of(peer)
    put(chip, join(choose(lower, mine, theirs), choose(lower, theirs, mine)))


def ring_kernel(position, m0, m1, m2, m3, plane, buf):
    mine = position(lax.axis_index("gz"))
    for k, got in zip(distances(lax.axis_index("gz")), (m0, m1, m2, m3)):
        buf[mine ^ k] = got[...]
    s = [parts_of(buf.at[j]) for j in range(4)]
    put(plane, join(join(s[0], s[1]), join(s[2], s[3])))


def descend(mine, s, ql, qr):
    lower, upper = join(s[0], s[1]), join(s[2], s[3])
    q = middle(lower, upper, ql, qr)
    up = mine // 2 == 1
    ql, qr = jnp.where(up, -q, ql), jnp.where(up, qr, q)
    q = middle(choose(up, s[2], s[0]), choose(up, s[3], s[1]), ql, qr)
    up = mine % 2 == 1
    return jnp.where(up, -q, ql), jnp.where(up, qr, q)


def finish_kernel(
    own, peer, c0, c1, c2, c3, p0, p1, p2, p3, local, gpz, gsz, out, cbuf, pbuf
):
    iy, ix = position_y(lax.axis_index("gz")), position_x(lax.axis_index("gz"))
    for k, (c, p) in zip(distances(lax.axis_index("gz")), ((c0, p0), (c1, p1), (c2, p2), (c3, p3))):
        cbuf[iy ^ k] = c[...]
        pbuf[ix ^ k] = p[...]
    column = [parts_of(cbuf.at[j]) for j in range(4)]
    whole = [parts_of(pbuf.at[j]) for j in range(4)]
    a, d, b, e, f = join(join(whole[0], whole[1]), join(whole[2], whole[3]))
    inv = 1.0 / (b * f - e * e)
    ql, qr = (e * d - f * a) * inv, (e * a - b * d) * inv
    ql, qr = descend(ix, whole, ql, qr)
    ql, qr = descend(iy, column, ql, qr)
    lower = lax.axis_index("gz") % 2 == 0
    mine, theirs = parts_of(own), parts_of(peer)
    q = middle(choose(lower, mine, theirs), choose(lower, theirs, mine), ql, qr)
    ql, qr = jnp.where(lower, ql, -q), jnp.where(lower, q, qr)
    planes = ql.shape[0]
    depth = out.shape[0] // planes
    for p in range(planes):
        i = p * depth
        out[i : i + depth, :] = (
            local[i : i + depth, :]
            + gsz[i : i + depth, :] * ql[p : p + 1, :]
            + gpz[i : i + depth, :] * qr[p : p + 1, :]
        )


def distances(z):
    core = z % 2
    return 0, 1, 3 - core, 2 + core


def chain_of(value, count, unit):
    far = lax.ppermute(value, "gz", [(i, i ^ ((3 - i % 2) * unit)) for i in range(count)])
    near = lax.ppermute(value, "gz", [(i, i ^ unit ^ 1) for i in range(count)])
    rest = lax.ppermute(far, "gz", [(i, i ^ 1) for i in range(count)])
    return [value, near, far, rest]


def position_y(z):
    return z // 2 % 4


def position_x(z):
    return z // 8


def partners(value, axis, count, unit):
    got = {
        k: lax.ppermute(value, axis, [(i, i ^ (k * unit) ^ (unit > 1)) for i in range(count)])
        for k in (1, 2, 3)
    }
    got[2] = got[2] * unity()
    return [got[k] for k in (1, 2, 3)]


def unity():
    return jnp.where(lax.axis_index("gz") < lax.axis_size("gz"), 1.0, 0.0)


def chip_neighbours(rows, peers):
    pairs = []
    for y in range(rows):
        for z in range(peers):
            end = z in (0, peers - 1)
            to = ((y ^ 1) * peers + z) if end else (y * peers + (z + 1 if z % 2 else z - 1))
            pairs.append((y * peers + z, to))
    return pairs


def shards(fields, cond_x, cond_y, cond_z, coupling):
    nf, nx, nz, ny = fields.shape
    planes, lines = nf * nx, nf * nx * nz
    peers = lax.axis_size("gz")
    steps = ny // SUB
    tall, flat, face, ends = (steps, SUB, lines), (lines, ny), (planes, ny), (5, planes, ny)
    hbm = pl.BlockSpec(memory_space=pltpu.HBM)
    dma = pltpu.SemaphoreType.DMA
    u, ky, kz, low, high, inner, outer = call(
        load_kernel, [flat] * 3 + [(2, *face)] * 4, [dma((3,))], 100_000, [hbm] * 3,
        fields.reshape(flat), cond_y.reshape(flat), cond_z.reshape(flat), vmem=53,
    )
    inner = lax.ppermute(inner, "gz", [(i, i ^ 1) for i in range(peers)])
    outer = lax.ppermute(outer, ("gy", "gz"), chip_neighbours(lax.axis_size("gy"), peers))
    gpy, gsy, ymat, gpz, gsz, zmat, r0 = call(
        factor_kernel,
        [tall, tall, (8, lines), flat, flat, (3, *face), flat],
        [(ny, lines)] + [tall] * 5 + [(nz, *face)],
        4_000_000,
        [VMEM] * 5,
        cond_x, coupling[None], u, ky, kz,
    )
    outer = outer * unity()
    msg, rt, ss, qq = call(
        functools.partial(y_ends_kernel, peers), [(8, lines), (ny, lines), tall, tall], [], 1_000_000, [VMEM] * 8,
        r0, low, high, inner, outer, gpy, gsy, ymat,
    )
    others = partners(msg, "gy", 4, 1)
    vloc, zends = call(
        functools.partial(y_local_kernel, peers), [tall, (3, *face)], [], 1_000_000, [VMEM] * 11,
        low, high, inner, outer, zmat, rt, ss, qq, gpy, gsy, ymat,
    )
    rz, own = call(
        y_finish_kernel, [flat, ends], [(4, 8, lines), (ny, lines)], 1_000_000, [VMEM] * 11,
        msg, *others, vloc, gpy, gsy, u, gpz, gsz, zends,
    )
    peer = lax.ppermute(own, "gz", [(i, i ^ 1) for i in range(peers)])
    local, ready = call(z_local_kernel, [flat, (8, 128)], [], 1_000_000, [VMEM] * 5, u, rz, gpz, gsz, zmat)
    [chip] = call(core_kernel, [ends], [], 50_000, [VMEM] * 3, own, peer, ready)
    column = chain_of(chip, peers, 2)
    [plane] = call(
        functools.partial(ring_kernel, position_y), [ends], [(4, *ends)], 50_000,
        [VMEM] * 4, *column,
    )
    whole = chain_of(plane, peers, 8)
    [out] = call(
        finish_kernel, [flat], [(4, *ends), (4, *ends)], 1_000_000, [VMEM] * 13,
        own, peer, *column, *whole, local, gpz, gsz,
    )
    return out.reshape(fields.shape)


def solution(mesh):
    block = P(None, None, "gz", "gy")
    return jax.shard_map(
        shards,
        mesh=mesh,
        in_specs=(block, P(), block, block, P()),
        out_specs=block,
        check_vma=False,
    )
```

```python
import functools

import jax
import jax.numpy as jnp
from jax import lax
from jax.experimental import pallas as pl
from jax.experimental.pallas import tpu as pltpu
from jax.sharding import PartitionSpec as P

SUB = 8
F32 = jnp.float32
VMEM = pl.BlockSpec(memory_space=pltpu.VMEM)
SMEM = pl.BlockSpec(memory_space=pltpu.SMEM)


def strided(ref, start, count, stride):
    return ref[pl.ds(start, count, stride=stride), :]


def load_kernel(uh, kyh, kzh, u, ky, kz, low, high, inner, outer, sem):
    copies = [
        pltpu.make_async_copy(src, dst, sem.at[i])
        for i, (src, dst) in enumerate(((uh, u), (kzh, kz), (kyh, ky)))
    ]
    for copy in copies:
        copy.start()
    planes = low.shape[1]
    depth = u.shape[0] // planes
    even = lax.axis_index("gz") % 2 == 0
    for i, array in enumerate((u, kz)):
        copies[i].wait()
        for p in range(planes):
            at = p * depth
            bottom, top = array[at : at + 1, :], array[at + depth - 1 : at + depth, :]
            low[i, p : p + 1, :] = bottom
            high[i, p : p + 1, :] = top
            inner[i, p : p + 1, :] = jnp.where(even, top, bottom)
            outer[i, p : p + 1, :] = jnp.where(even, bottom, top)
    copies[2].wait()


def factor_kernel(
    cx, cp, u, ky, kz, gpy, gsy, ymat, gpz, gsz, zmat, r0, kt, zr, wa, wb, wc, wd, zz
):
    lines, length = ky.shape
    steps = length // SUB
    planes, depth = zmat.shape[1], lines // zmat.shape[1]
    kt[...] = ky[...].T
    first = strided(kt, 0, SUB, steps)
    here = first
    for t in range(steps):
        after = strided(kt, t + 1, SUB, steps) if t + 1 < steps else pltpu.roll(first, SUB - 1, 0)
        zr[t] = 4.0 / (here + after)
        here = after
    last = strided(kt, steps - 1, SUB, steps)
    row = lax.broadcasted_iota(jnp.int32, (SUB, lines), 0)
    one, zero = jnp.ones((SUB, lines), F32), jnp.zeros((SUB, lines), F32)
    aw, aj, bw, bj = one, zero, zero, one
    for t in range(steps):
        wa[t], wb[t] = aw, bw
        aj, bj = aj + aw, bj + bw
        aw, bw = aw + zr[t] * aj, bw + zr[t] * bj
    cw, cj, dw, dj = one, zero, zero, one
    for t in reversed(range(steps)):
        wc[t], wd[t] = cw, dw
        cj, dj = cj + cw, dj + dw
        z = zr[t - 1] if t else pltpu.roll(zr[steps - 1], 1, 0)
        cw, dw = cw + z * cj, dw + z * dj
    al, be, ga, de = one, zero, one, zero
    for j in range(SUB - 1):
        nal, nbe = pltpu.roll(aw * al + bw * be, 1, 0), pltpu.roll(aj * al + bj * be, 1, 0)
        al, be = jnp.where(row == j + 1, nal, al), jnp.where(row == j + 1, nbe, be)
        nga = pltpu.roll(cw * ga + dw * de, SUB - 1, 0)
        nde = pltpu.roll(cj * ga + dj * de, SUB - 1, 0)
        at = SUB - 2 - j
        ga, de = jnp.where(row == at, nga, ga), jnp.where(row == at, nde, de)
    iw = 1.0 / (aj * al + bj * be)[SUB - 1 :, :]
    iv = 1.0 / (cj * ga + dj * de)[:1, :]
    al, be, ga, de = al * iw, be * iw, ga * iv, de * iv
    for t in range(steps):
        gpy[t] = al * wa[t] + be * wb[t]
        gsy[t] = ga * wc[t] + de * wd[t]
    ymat[...] = jnp.zeros_like(ymat)
    ymat[2:3, :] = gsy[0][:1, :]
    ymat[3:4, :] = iw
    ymat[4:5, :] = gpy[steps - 1][SUB - 1 :, :]
    ymat[5:6, :] = first[:1, :]
    ymat[6:7, :] = last[SUB - 1 :, :]
    here = [kz[pl.ds(p * depth, 1), :] for p in range(planes)]
    here = jnp.concatenate(here, 0)
    for t in range(depth - 1):
        after = jnp.concatenate([kz[pl.ds(p * depth + t + 1, 1), :] for p in range(planes)], 0)
        zz[t] = 4.0 / (here + after)
        here = after
    w, j = jnp.ones_like(here), jnp.zeros_like(here)
    ws = []
    for t in range(depth):
        ws.append(w)
        j = j + w
        if t + 1 < depth:
            w = w + zz[t] * j
    ij = 1.0 / j
    for t in range(depth):
        g = ws[t] * ij
        for p in range(planes):
            gpz[pl.ds(p * depth + t, 1), :] = g[p : p + 1, :]
    zmat[1] = ij
    zmat[2] = ws[depth - 1] * ij
    w, j = jnp.ones_like(here), jnp.zeros_like(here)
    ws = []
    for t in reversed(range(depth)):
        ws.append(w)
        j = j + w
        if t:
            w = w + zz[t - 1] * j
    ij = 1.0 / j
    for t in range(depth):
        g = ws[depth - 1 - t] * ij
        for p in range(planes):
            gsz[pl.ds(p * depth + t, 1), :] = g[p : p + 1, :]
    zmat[0] = ws[depth - 1] * ij
    for f in range(2):
        for x in range(2):
            at = (f * 2 + x) * depth
            me = u[at : at + depth, :]
            beside = u[(f * 2 + 1 - x) * depth : (f * 2 + 2 - x) * depth, :]
            other = u[((1 - f) * 2 + x) * depth : ((1 - f) * 2 + x + 1) * depth, :]
            face = 0.5 * (cx[f : f + 1, 0:1] + cx[f : f + 1, 1:2])
            k = kz[at : at + depth, :]
            flux = 0.5 * (k[1:] + k[:-1]) * (me[1:] - me[:-1])
            none = jnp.zeros((1, length), F32)
            flow = jnp.concatenate([flux, none], 0) - jnp.concatenate([none, flux], 0)
            r0[at : at + depth, :] = (
                (2.0 - 0.5 * cx[f : f + 1, x : x + 1]) * me
                + face * (beside - me)
                + cp[:, x : x + 1] * (other - me)
                + flow
            )


def y_base_kernel(r0, gpy, gsy, ymat, base, gp_edge, gs_edge, gp_rows, gs_rows, rt):
    steps, _, lines = gpy.shape
    planes = gp_edge.shape[0] // 2
    depth = lines // planes
    rt[...] = r0[...].T
    s = jnp.zeros((SUB, lines), F32)
    q = jnp.zeros((SUB, lines), F32)
    for t in range(steps):
        r = strided(rt, t, SUB, steps)
        s, q = s + gpy[t] * r, q + gsy[t] * r
    base[...] = ymat[...]
    base[0:1, :] = jnp.sum(q, axis=0, keepdims=True)
    base[1:2, :] = jnp.sum(s, axis=0, keepdims=True)
    for g, edge, rows in ((gpy, gp_edge, gp_rows), (gsy, gs_edge, gs_rows)):
        for t in range(steps):
            rt[pl.ds(t, SUB, stride=steps), :] = g[t]
        rows[...] = rt[...].T
        for p in range(planes):
            edge[p : p + 1, :] = rows[p * depth : p * depth + 1]
            edge[planes + p : planes + p + 1, :] = rows[(p + 1) * depth - 1 : (p + 1) * depth]


def y_ends_kernel(peers, low, high, inner, outer, base, gp_edge, gs_edge, msg, change):
    planes, lines = low.shape[1], base.shape[1]
    depth = lines // planes
    under = jnp.where(lax.axis_index("gz") > 0, 1.0, 0.0)
    over = jnp.where(lax.axis_index("gz") < peers - 1, 1.0, 0.0)
    even = lax.axis_index("gz") % 2 == 0
    below = [jnp.where(even, outer[i], inner[i]) * under for i in range(2)]
    above = [jnp.where(even, inner[i], outer[i]) * over for i in range(2)]
    lo = 0.5 * (below[1] + low[1]) * (below[0] - low[0])
    hi = 0.5 * (above[1] + high[1]) * (above[0] - high[0])
    both = jnp.concatenate([lo, hi], 0)
    change[...] = both
    row = lax.broadcasted_iota(jnp.int32, (2 * planes, lines), 0)
    line = lax.broadcasted_iota(jnp.int32, (2 * planes, lines), 1)
    here = line == jnp.where(row < planes, row * depth, (row - planes + 1) * depth - 1)
    msg[...] = base[...]
    for i, edge in enumerate((gs_edge, gp_edge)):
        ends = jnp.sum(edge[...] * both, axis=1, keepdims=True)
        added = jnp.sum(jnp.where(here, ends, 0.0), axis=0, keepdims=True)
        msg[i : i + 1, :] = base[i : i + 1, :] + added


def y_local_kernel(
    peers, u, r0, change, low, high, inner, outer, zmat, gpy, gsy, ymat, rz0, zends, rt, ss, qq
):
    steps, _, lines = gpy.shape
    planes, length = low.shape[1:]
    depth = lines // planes
    row = lax.broadcasted_iota(jnp.int32, (SUB, length), 0)
    parts = []
    for p in range(planes):
        i = p * depth
        top, mid, end = r0[i : i + SUB], r0[i + SUB : i + depth - SUB], r0[i + depth - SUB : i + depth]
        parts += [
            jnp.where(row == 0, top + change[p : p + 1, :], top),
            mid,
            jnp.where(row == SUB - 1, end + change[planes + p : planes + p + 1, :], end),
        ]
    rt[...] = jnp.concatenate(parts, 0).T
    s = jnp.zeros((SUB, lines), F32)
    q = jnp.zeros((SUB, lines), F32)
    for t in range(steps):
        back = steps - 1 - t
        s = s + gpy[t] * strided(rt, t, SUB, steps)
        ss[t] = s
        qq[back] = q
        q = q + gsy[back] * strided(rt, back, SUB, steps)
    row = lax.broadcasted_iota(jnp.int32, (SUB, lines), 0)
    so, qo = jnp.zeros_like(s), jnp.zeros_like(q)
    for j in range(1, SUB):
        so = so + jnp.where(row >= j, pltpu.roll(s, j, 0), 0.0)
        qo = qo + jnp.where(row < SUB - j, pltpu.roll(q, SUB - j, 0), 0.0)
    w = 1.0 / ymat[3:4, :]
    for t in range(steps):
        rt[pl.ds(t, SUB, stride=steps), :] = gsy[t] * w * (ss[t] + so) + gpy[t] * w * (qq[t] + qo)
    rz0[...] = rt[...].T - 2.0 * u[...]
    under = jnp.where(lax.axis_index("gz") > 0, 0.0, 1.0)
    over = jnp.where(lax.axis_index("gz") < peers - 1, 1.0, 0.0)
    zends[0] = zmat[0] + under * 4.0 / low[1]
    zends[1] = zmat[1]
    above = jnp.where(lax.axis_index("gz") % 2 == 0, inner[1], outer[1])
    zends[2] = zmat[2] + 4.0 / (above * over + high[1])


def y_finish_kernel(m0, m1, m2, m3, rz0, gp_rows, gs_rows, gpz, gsz, zends, rz, own, buf):
    lines = m0.shape[1]
    planes = own.shape[1]
    depth = lines // planes
    got = (m0, m1, m2, m3)
    mine = lax.axis_index("gy")
    for k in range(4):
        buf[mine ^ k] = got[k][...]
    seg = []
    for j in range(4):
        s = buf[j]
        seg.append([s[i : i + 1, :] for i in range(7)])
    zero = jnp.zeros((1, lines), F32)
    gap = [4.0 / (seg[j][6] + seg[j + 1][5]) for j in range(3)]
    e, r = zero, 4.0 / seg[0][5]
    el, rl = e, r
    for j in range(3):
        a, d, b, c, f = seg[j][:5]
        inv = 1.0 / (r + b)
        e, r = d + c * (e - a) * inv, f - c * c * inv + gap[j]
        el, rl = jnp.where(mine == j + 1, e, el), jnp.where(mine == j + 1, r, rl)
    e, r = zero, 4.0 / seg[3][6]
    er, rr = e, r
    for j in (3, 2, 1):
        a, d, b, c, f = seg[j][:5]
        inv = 1.0 / (r + f)
        e, r = a + c * (e - d) * inv, b - c * c * inv + gap[j - 1]
        er, rr = jnp.where(mine == j - 1, e, er), jnp.where(mine == j - 1, r, rr)
    a, d, b, c, f = [m0[i : i + 1, :] for i in range(5)]
    left, right = b + rl, f + rr
    inv = 1.0 / (left * right - c * c)
    ql = ((el - a) * right - c * (er - d)) * inv
    qr = ((er - d) * left - c * (el - a)) * inv
    flux = jnp.concatenate([ql, qr, jnp.zeros((6, lines), F32)], 0).T
    for p in range(planes):
        rows = slice(p * depth, (p + 1) * depth)
        r = rz0[rows, :] + gs_rows[rows, :] * flux[rows, 0:1] + gp_rows[rows, :] * flux[rows, 1:2]
        rz[rows, :] = r
        own[0, p : p + 1, :] = jnp.sum(gsz[rows, :] * r, axis=0, keepdims=True)
        own[1, p : p + 1, :] = jnp.sum(gpz[rows, :] * r, axis=0, keepdims=True)
    for i in range(3):
        own[i + 2] = zends[i]


def z_local_kernel(u, rz, gpz, gsz, zmat, out, ready):
    ready[...] = jnp.zeros_like(ready)
    _, planes, length = zmat.shape
    depth = rz.shape[0] // planes
    for p in range(planes):
        w = 1.0 / zmat[1, p : p + 1, :]
        s = jnp.zeros((1, length), F32)
        ss = []
        for t in range(depth):
            at = pl.ds(p * depth + t, 1)
            s = s + gpz[at, :] * rz[at, :]
            ss.append(s)
        q = jnp.zeros((1, length), F32)
        for t in reversed(range(depth)):
            at = pl.ds(p * depth + t, 1)
            out[at, :] = u[at, :] + w * (gsz[at, :] * ss[t] + gpz[at, :] * q)
            q = q + gsz[at, :] * rz[at, :]


def call(kernel, outs, scratch, cost, in_specs, *args, vmem=32):
    return pl.pallas_call(
        kernel,
        out_shape=[jax.ShapeDtypeStruct(s, F32) for s in outs],
        in_specs=in_specs,
        out_specs=[VMEM] * len(outs),
        scratch_shapes=[pltpu.VMEM(s, F32) if isinstance(s, tuple) else s for s in scratch],
        compiler_params=pltpu.CompilerParams(vmem_limit_bytes=int(vmem * 2**20)),
        cost_estimate=pl.CostEstimate(flops=cost, bytes_accessed=cost // 4, transcendentals=0),
    )(*args)


def join(s, t):
    a1, d1, b1, e1, f1 = s
    a2, d2, b2, e2, f2 = t
    inv = 1.0 / (f1 + b2)
    jump = (a2 - d1) * inv
    cross = e1 * inv
    return (
        a1 + e1 * jump,
        d2 - e2 * jump,
        b1 - e1 * cross,
        e2 * cross,
        f2 - e2 * e2 * inv,
    )


def middle(s, t, ql, qr):
    return (t[0] - s[1] + t[3] * qr - s[3] * ql) / (s[4] + t[2])


def parts_of(ref):
    return tuple(ref[i] for i in range(5))


def choose(flag, s, t):
    return tuple(jnp.where(flag, a, b) for a, b in zip(s, t))


def put(ref, value):
    for i in range(5):
        ref[i] = value[i]


def core_kernel(own, peer, ready, chip):
    lower = lax.axis_index("gz") % 2 == 0
    mine, theirs = parts_of(own), parts_of(peer)
    put(chip, join(choose(lower, mine, theirs), choose(lower, theirs, mine)))


def ring_kernel(position, m0, m1, m2, m3, plane, buf):
    mine = position(lax.axis_index("gz"))
    for k, got in zip(distances(lax.axis_index("gz")), (m0, m1, m2, m3)):
        buf[mine ^ k] = got[...]
    s = [parts_of(buf.at[j]) for j in range(4)]
    put(plane, join(join(s[0], s[1]), join(s[2], s[3])))


def descend(mine, s, ql, qr):
    lower, upper = join(s[0], s[1]), join(s[2], s[3])
    q = middle(lower, upper, ql, qr)
    up = mine // 2 == 1
    ql, qr = jnp.where(up, -q, ql), jnp.where(up, qr, q)
    q = middle(choose(up, s[2], s[0]), choose(up, s[3], s[1]), ql, qr)
    up = mine % 2 == 1
    return jnp.where(up, -q, ql), jnp.where(up, qr, q)


def finish_kernel(
    own, peer, c0, c1, c2, c3, p0, p1, p2, p3, local, gpz, gsz, out, cbuf, pbuf
):
    iy, ix = position_y(lax.axis_index("gz")), position_x(lax.axis_index("gz"))
    for k, (c, p) in zip(distances(lax.axis_index("gz")), ((c0, p0), (c1, p1), (c2, p2), (c3, p3))):
        cbuf[iy ^ k] = c[...]
        pbuf[ix ^ k] = p[...]
    column = [parts_of(cbuf.at[j]) for j in range(4)]
    whole = [parts_of(pbuf.at[j]) for j in range(4)]
    a, d, b, e, f = join(join(whole[0], whole[1]), join(whole[2], whole[3]))
    inv = 1.0 / (b * f - e * e)
    ql, qr = (e * d - f * a) * inv, (e * a - b * d) * inv
    ql, qr = descend(ix, whole, ql, qr)
    ql, qr = descend(iy, column, ql, qr)
    lower = lax.axis_index("gz") % 2 == 0
    mine, theirs = parts_of(own), parts_of(peer)
    q = middle(choose(lower, mine, theirs), choose(lower, theirs, mine), ql, qr)
    ql, qr = jnp.where(lower, ql, -q), jnp.where(lower, q, qr)
    planes = ql.shape[0]
    depth = out.shape[0] // planes
    for p in range(planes):
        i = p * depth
        out[i : i + depth, :] = (
            local[i : i + depth, :]
            + gsz[i : i + depth, :] * ql[p : p + 1, :]
            + gpz[i : i + depth, :] * qr[p : p + 1, :]
        )


def distances(z):
    core = z % 2
    return 0, 1, 3 - core, 2 + core


def chain_of(value, count, unit):
    far = lax.ppermute(value, "gz", [(i, i ^ ((3 - i % 2) * unit)) for i in range(count)])
    near = lax.ppermute(value, "gz", [(i, i ^ unit ^ 1) for i in range(count)])
    rest = lax.ppermute(far, "gz", [(i, i ^ 1) for i in range(count)])
    return [value, near, far, rest]


def position_y(z):
    return z // 2 % 4


def position_x(z):
    return z // 8


def partners(value, axis, count, unit):
    got = {
        k: lax.ppermute(value, axis, [(i, i ^ (k * unit) ^ (unit > 1)) for i in range(count)])
        for k in (1, 2, 3)
    }
    got[2], got[3] = got[2] * unity(), got[3] * unity()
    got[2] = lax.optimization_barrier(got[2]) * unity()
    return [got[k] for k in (1, 2, 3)]


def unity():
    return jnp.where(lax.axis_index("gz") < lax.axis_size("gz"), 1.0, 0.0)


def chip_neighbours(rows, peers):
    pairs = []
    for y in range(rows):
        for z in range(peers):
            end = z in (0, peers - 1)
            to = ((y ^ 1) * peers + z) if end else (y * peers + (z + 1 if z % 2 else z - 1))
            pairs.append((y * peers + z, to))
    return pairs


def shards(fields, cond_x, cond_y, cond_z, coupling):
    nf, nx, nz, ny = fields.shape
    planes, lines = nf * nx, nf * nx * nz
    peers = lax.axis_size("gz")
    steps = ny // SUB
    tall, flat, face, ends = (steps, SUB, lines), (lines, ny), (planes, ny), (5, planes, ny)
    hbm = pl.BlockSpec(memory_space=pltpu.HBM)
    dma = pltpu.SemaphoreType.DMA
    u, ky, kz, low, high, inner, outer = call(
        load_kernel, [flat] * 3 + [(2, *face)] * 4, [dma((3,))], 100_000, [hbm] * 3,
        fields.reshape(flat), cond_y.reshape(flat), cond_z.reshape(flat), vmem=53,
    )
    inner = lax.ppermute(inner, "gz", [(i, i ^ 1) for i in range(peers)])
    outer = lax.ppermute(outer, ("gy", "gz"), chip_neighbours(lax.axis_size("gy"), peers))
    gpy, gsy, ymat, gpz, gsz, zmat, r0 = call(
        factor_kernel,
        [tall, tall, (8, lines), flat, flat, (3, *face), flat],
        [(ny, lines)] + [tall] * 5 + [(nz, *face)],
        4_000_000,
        [VMEM] * 5,
        cond_x, coupling[None], u, ky, kz,
    )
    base, gp_edge, gs_edge, gp_rows, gs_rows = call(
        y_base_kernel, [(8, lines)] + [(2 * planes, ny)] * 2 + [flat] * 2, [(ny, lines)], 1_000_000, [VMEM] * 4,
        r0, gpy, gsy, ymat,
    )
    outer = outer * unity()
    msg, change = call(
        functools.partial(y_ends_kernel, peers), [(8, lines), (2 * planes, ny)], [], 100_000,
        [VMEM] * 7,
        low, high, inner, outer, base, gp_edge, gs_edge,
    )
    others = partners(msg, "gy", 4, 1)
    rz0, zends = call(
        functools.partial(y_local_kernel, peers), [flat, (3, *face)], [(ny, lines), tall, tall],
        1_000_000, [VMEM] * 11,
        u, r0, change, low, high, inner, outer, zmat, gpy, gsy, ymat,
    )
    rz, own = call(
        y_finish_kernel, [flat, ends], [(4, 8, lines)], 1_000_000, [VMEM] * 10,
        msg, *others, rz0, gp_rows, gs_rows, gpz, gsz, zends,
    )
    peer = lax.ppermute(own, "gz", [(i, i ^ 1) for i in range(peers)])
    local, ready = call(z_local_kernel, [flat, (8, 128)], [], 1_000_000, [VMEM] * 5, u, rz, gpz, gsz, zmat)
    [chip] = call(core_kernel, [ends], [], 50_000, [VMEM] * 3, own, peer, ready)
    column = chain_of(chip, peers, 2)
    [plane] = call(
        functools.partial(ring_kernel, position_y), [ends], [(4, *ends)], 50_000,
        [VMEM] * 4, *column,
    )
    whole = chain_of(plane, peers, 8)
    [out] = call(
        finish_kernel, [flat], [(4, *ends), (4, *ends)], 1_000_000, [VMEM] * 13,
        own, peer, *column, *whole, local, gpz, gsz,
    )
    return out.reshape(fields.shape)


def solution(mesh):
    block = P(None, None, "gz", "gy")
    return jax.shard_map(
        shards,
        mesh=mesh,
        in_specs=(block, P(), block, block, P()),
        out_specs=block,
        check_vma=False,
    )
```

```python
import functools

import jax
import jax.numpy as jnp
from jax import lax
from jax.experimental import pallas as pl
from jax.experimental.pallas import tpu as pltpu
from jax.sharding import PartitionSpec as P

SUB = 8
F32 = jnp.float32
VMEM = pl.BlockSpec(memory_space=pltpu.VMEM)
SMEM = pl.BlockSpec(memory_space=pltpu.SMEM)


def strided(ref, start, count, stride):
    return ref[pl.ds(start, count, stride=stride), :]


def load_kernel(uh, kyh, kzh, u, ky, kz, low, high, inner, outer, sem):
    copies = [
        pltpu.make_async_copy(src, dst, sem.at[i])
        for i, (src, dst) in enumerate(((uh, u), (kzh, kz), (kyh, ky)))
    ]
    for copy in copies:
        copy.start()
    planes = low.shape[1]
    depth = u.shape[0] // planes
    even = lax.axis_index("gz") % 2 == 0
    for i, array in enumerate((u, kz)):
        copies[i].wait()
        for p in range(planes):
            at = p * depth
            bottom, top = array[at : at + 1, :], array[at + depth - 1 : at + depth, :]
            low[i, p : p + 1, :] = bottom
            high[i, p : p + 1, :] = top
            inner[i, p : p + 1, :] = jnp.where(even, top, bottom)
            outer[i, p : p + 1, :] = jnp.where(even, bottom, top)
    copies[2].wait()


def factor_kernel(
    cx, cp, u, ky, kz, gpy, gsy, ymat, gpz, gsz, zmat, r0, kt, zr, wa, wb, wc, wd, zz
):
    lines, length = ky.shape
    steps = length // SUB
    planes, depth = zmat.shape[1], lines // zmat.shape[1]
    kt[...] = ky[...].T
    first = strided(kt, 0, SUB, steps)
    here = first
    for t in range(steps):
        after = strided(kt, t + 1, SUB, steps) if t + 1 < steps else pltpu.roll(first, SUB - 1, 0)
        zr[t] = 4.0 / (here + after)
        here = after
    last = strided(kt, steps - 1, SUB, steps)
    row = lax.broadcasted_iota(jnp.int32, (SUB, lines), 0)
    one, zero = jnp.ones((SUB, lines), F32), jnp.zeros((SUB, lines), F32)
    aw, aj, bw, bj = one, zero, zero, one
    for t in range(steps):
        wa[t], wb[t] = aw, bw
        aj, bj = aj + aw, bj + bw
        aw, bw = aw + zr[t] * aj, bw + zr[t] * bj
    cw, cj, dw, dj = one, zero, zero, one
    for t in reversed(range(steps)):
        wc[t], wd[t] = cw, dw
        cj, dj = cj + cw, dj + dw
        z = zr[t - 1] if t else pltpu.roll(zr[steps - 1], 1, 0)
        cw, dw = cw + z * cj, dw + z * dj
    al, be, ga, de = one, zero, one, zero
    for j in range(SUB - 1):
        nal, nbe = pltpu.roll(aw * al + bw * be, 1, 0), pltpu.roll(aj * al + bj * be, 1, 0)
        al, be = jnp.where(row == j + 1, nal, al), jnp.where(row == j + 1, nbe, be)
        nga = pltpu.roll(cw * ga + dw * de, SUB - 1, 0)
        nde = pltpu.roll(cj * ga + dj * de, SUB - 1, 0)
        at = SUB - 2 - j
        ga, de = jnp.where(row == at, nga, ga), jnp.where(row == at, nde, de)
    iw = 1.0 / (aj * al + bj * be)[SUB - 1 :, :]
    iv = 1.0 / (cj * ga + dj * de)[:1, :]
    al, be, ga, de = al * iw, be * iw, ga * iv, de * iv
    for t in range(steps):
        gpy[t] = al * wa[t] + be * wb[t]
        gsy[t] = ga * wc[t] + de * wd[t]
    ymat[...] = jnp.zeros_like(ymat)
    ymat[2:3, :] = gsy[0][:1, :]
    ymat[3:4, :] = iw
    ymat[4:5, :] = gpy[steps - 1][SUB - 1 :, :]
    ymat[5:6, :] = first[:1, :]
    ymat[6:7, :] = last[SUB - 1 :, :]
    here = [kz[pl.ds(p * depth, 1), :] for p in range(planes)]
    here = jnp.concatenate(here, 0)
    for t in range(depth - 1):
        after = jnp.concatenate([kz[pl.ds(p * depth + t + 1, 1), :] for p in range(planes)], 0)
        zz[t] = 4.0 / (here + after)
        here = after
    w, j = jnp.ones_like(here), jnp.zeros_like(here)
    ws = []
    for t in range(depth):
        ws.append(w)
        j = j + w
        if t + 1 < depth:
            w = w + zz[t] * j
    ij = 1.0 / j
    for t in range(depth):
        g = ws[t] * ij
        for p in range(planes):
            gpz[pl.ds(p * depth + t, 1), :] = g[p : p + 1, :]
    zmat[1] = ij
    zmat[2] = ws[depth - 1] * ij
    w, j = jnp.ones_like(here), jnp.zeros_like(here)
    ws = []
    for t in reversed(range(depth)):
        ws.append(w)
        j = j + w
        if t:
            w = w + zz[t - 1] * j
    ij = 1.0 / j
    for t in range(depth):
        g = ws[depth - 1 - t] * ij
        for p in range(planes):
            gsz[pl.ds(p * depth + t, 1), :] = g[p : p + 1, :]
    zmat[0] = ws[depth - 1] * ij
    for f in range(2):
        for x in range(2):
            at = (f * 2 + x) * depth
            me = u[at : at + depth, :]
            beside = u[(f * 2 + 1 - x) * depth : (f * 2 + 2 - x) * depth, :]
            other = u[((1 - f) * 2 + x) * depth : ((1 - f) * 2 + x + 1) * depth, :]
            face = 0.5 * (cx[f : f + 1, 0:1] + cx[f : f + 1, 1:2])
            k = kz[at : at + depth, :]
            flux = 0.5 * (k[1:] + k[:-1]) * (me[1:] - me[:-1])
            none = jnp.zeros((1, length), F32)
            flow = jnp.concatenate([flux, none], 0) - jnp.concatenate([none, flux], 0)
            r0[at : at + depth, :] = (
                (2.0 - 0.5 * cx[f : f + 1, x : x + 1]) * me
                + face * (beside - me)
                + cp[:, x : x + 1] * (other - me)
                + flow
            )


def y_base_kernel(r0, gpy, gsy, ymat, base, gp_edge, gs_edge, gp_rows, gs_rows, rt):
    steps, _, lines = gpy.shape
    planes = gp_edge.shape[0] // 2
    depth = lines // planes
    rt[...] = r0[...].T
    s = jnp.zeros((SUB, lines), F32)
    q = jnp.zeros((SUB, lines), F32)
    for t in range(steps):
        r = strided(rt, t, SUB, steps)
        s, q = s + gpy[t] * r, q + gsy[t] * r
    base[...] = ymat[...]
    base[0:1, :] = jnp.sum(q, axis=0, keepdims=True)
    base[1:2, :] = jnp.sum(s, axis=0, keepdims=True)
    for g, edge, rows in ((gpy, gp_edge, gp_rows), (gsy, gs_edge, gs_rows)):
        for t in range(steps):
            rt[pl.ds(t, SUB, stride=steps), :] = g[t]
        rows[...] = rt[...].T
        for p in range(planes):
            edge[p : p + 1, :] = rows[p * depth : p * depth + 1]
            edge[planes + p : planes + p + 1, :] = rows[(p + 1) * depth - 1 : (p + 1) * depth]


def y_ends_kernel(peers, low, high, inner, outer, base, gp_edge, gs_edge, msg, change):
    planes, lines = low.shape[1], base.shape[1]
    depth = lines // planes
    under = jnp.where(lax.axis_index("gz") > 0, 1.0, 0.0)
    over = jnp.where(lax.axis_index("gz") < peers - 1, 1.0, 0.0)
    even = lax.axis_index("gz") % 2 == 0
    below = [jnp.where(even, outer[i], inner[i]) * under for i in range(2)]
    above = [jnp.where(even, inner[i], outer[i]) * over for i in range(2)]
    lo = 0.5 * (below[1] + low[1]) * (below[0] - low[0])
    hi = 0.5 * (above[1] + high[1]) * (above[0] - high[0])
    both = jnp.concatenate([lo, hi], 0)
    change[...] = both
    row = lax.broadcasted_iota(jnp.int32, (2 * planes, lines), 0)
    line = lax.broadcasted_iota(jnp.int32, (2 * planes, lines), 1)
    here = line == jnp.where(row < planes, row * depth, (row - planes + 1) * depth - 1)
    msg[...] = base[...]
    for i, edge in enumerate((gs_edge, gp_edge)):
        ends = jnp.sum(edge[...] * both, axis=1, keepdims=True)
        added = jnp.sum(jnp.where(here, ends, 0.0), axis=0, keepdims=True)
        msg[i : i + 1, :] = base[i : i + 1, :] + added


def y_local_kernel(
    peers, u, r0, change, low, high, inner, outer, zmat, gpy, gsy, ymat, rz0, zends, rt, ss, qq
):
    steps, _, lines = gpy.shape
    planes, length = low.shape[1:]
    depth = lines // planes
    row = lax.broadcasted_iota(jnp.int32, (SUB, length), 0)
    parts = []
    for p in range(planes):
        i = p * depth
        top, mid, end = r0[i : i + SUB], r0[i + SUB : i + depth - SUB], r0[i + depth - SUB : i + depth]
        parts += [
            jnp.where(row == 0, top + change[p : p + 1, :], top),
            mid,
            jnp.where(row == SUB - 1, end + change[planes + p : planes + p + 1, :], end),
        ]
    rt[...] = jnp.concatenate(parts, 0).T
    s = jnp.zeros((SUB, lines), F32)
    q = jnp.zeros((SUB, lines), F32)
    for t in range(steps):
        back = steps - 1 - t
        s = s + gpy[t] * strided(rt, t, SUB, steps)
        ss[t] = s
        qq[back] = q
        q = q + gsy[back] * strided(rt, back, SUB, steps)
    row = lax.broadcasted_iota(jnp.int32, (SUB, lines), 0)
    so, qo = jnp.zeros_like(s), jnp.zeros_like(q)
    for j in range(1, SUB):
        so = so + jnp.where(row >= j, pltpu.roll(s, j, 0), 0.0)
        qo = qo + jnp.where(row < SUB - j, pltpu.roll(q, SUB - j, 0), 0.0)
    w = 1.0 / ymat[3:4, :]
    for t in range(steps):
        rt[pl.ds(t, SUB, stride=steps), :] = gsy[t] * w * (ss[t] + so) + gpy[t] * w * (qq[t] + qo)
    rz0[...] = rt[...].T - 2.0 * u[...]
    under = jnp.where(lax.axis_index("gz") > 0, 0.0, 1.0)
    over = jnp.where(lax.axis_index("gz") < peers - 1, 1.0, 0.0)
    zends[0] = zmat[0] + under * 4.0 / low[1]
    zends[1] = zmat[1]
    above = jnp.where(lax.axis_index("gz") % 2 == 0, inner[1], outer[1])
    zends[2] = zmat[2] + 4.0 / (above * over + high[1])


def y_finish_kernel(m0, m1, m2, m3, rz0, gp_rows, gs_rows, gpz, gsz, zends, rz, own, buf):
    lines = m0.shape[1]
    planes = own.shape[1]
    depth = lines // planes
    got = (m0, m1, m2, m3)
    mine = lax.axis_index("gy")
    for k in range(4):
        buf[mine ^ k] = got[k][...]
    seg = []
    for j in range(4):
        s = buf[j]
        seg.append([s[i : i + 1, :] for i in range(7)])
    zero = jnp.zeros((1, lines), F32)
    gap = [4.0 / (seg[j][6] + seg[j + 1][5]) for j in range(3)]
    e, r = zero, 4.0 / seg[0][5]
    el, rl = e, r
    for j in range(3):
        a, d, b, c, f = seg[j][:5]
        inv = 1.0 / (r + b)
        e, r = d + c * (e - a) * inv, f - c * c * inv + gap[j]
        el, rl = jnp.where(mine == j + 1, e, el), jnp.where(mine == j + 1, r, rl)
    e, r = zero, 4.0 / seg[3][6]
    er, rr = e, r
    for j in (3, 2, 1):
        a, d, b, c, f = seg[j][:5]
        inv = 1.0 / (r + f)
        e, r = a + c * (e - d) * inv, b - c * c * inv + gap[j - 1]
        er, rr = jnp.where(mine == j - 1, e, er), jnp.where(mine == j - 1, r, rr)
    a, d, b, c, f = [m0[i : i + 1, :] for i in range(5)]
    left, right = b + rl, f + rr
    inv = 1.0 / (left * right - c * c)
    ql = ((el - a) * right - c * (er - d)) * inv
    qr = ((er - d) * left - c * (el - a)) * inv
    flux = jnp.concatenate([ql, qr, jnp.zeros((6, lines), F32)], 0).T
    for p in range(planes):
        rows = slice(p * depth, (p + 1) * depth)
        r = rz0[rows, :] + gs_rows[rows, :] * flux[rows, 0:1] + gp_rows[rows, :] * flux[rows, 1:2]
        rz[rows, :] = r
        own[0, p : p + 1, :] = jnp.sum(gsz[rows, :] * r, axis=0, keepdims=True)
        own[1, p : p + 1, :] = jnp.sum(gpz[rows, :] * r, axis=0, keepdims=True)
    for i in range(3):
        own[i + 2] = zends[i]


def z_local_kernel(u, rz, gpz, gsz, zmat, out, ready):
    ready[...] = jnp.zeros_like(ready)
    _, planes, length = zmat.shape
    depth = rz.shape[0] // planes
    for p in range(planes):
        w = 1.0 / zmat[1, p : p + 1, :]
        s = jnp.zeros((1, length), F32)
        ss = []
        for t in range(depth):
            at = pl.ds(p * depth + t, 1)
            s = s + gpz[at, :] * rz[at, :]
            ss.append(s)
        q = jnp.zeros((1, length), F32)
        for t in reversed(range(depth)):
            at = pl.ds(p * depth + t, 1)
            out[at, :] = u[at, :] + w * (gsz[at, :] * ss[t] + gpz[at, :] * q)
            q = q + gsz[at, :] * rz[at, :]


def call(kernel, outs, scratch, cost, in_specs, *args, vmem=32):
    return pl.pallas_call(
        kernel,
        out_shape=[jax.ShapeDtypeStruct(s, F32) for s in outs],
        in_specs=in_specs,
        out_specs=[VMEM] * len(outs),
        scratch_shapes=[pltpu.VMEM(s, F32) if isinstance(s, tuple) else s for s in scratch],
        compiler_params=pltpu.CompilerParams(vmem_limit_bytes=int(vmem * 2**20)),
        cost_estimate=pl.CostEstimate(flops=cost, bytes_accessed=cost // 4, transcendentals=0),
    )(*args)


def join(s, t):
    a1, d1, b1, e1, f1 = s
    a2, d2, b2, e2, f2 = t
    inv = 1.0 / (f1 + b2)
    jump = (a2 - d1) * inv
    cross = e1 * inv
    return (
        a1 + e1 * jump,
        d2 - e2 * jump,
        b1 - e1 * cross,
        e2 * cross,
        f2 - e2 * e2 * inv,
    )


def middle(s, t, ql, qr):
    return (t[0] - s[1] + t[3] * qr - s[3] * ql) / (s[4] + t[2])


def parts_of(ref):
    return tuple(ref[i] for i in range(5))


def choose(flag, s, t):
    return tuple(jnp.where(flag, a, b) for a, b in zip(s, t))


def put(ref, value):
    for i in range(5):
        ref[i] = value[i]


def core_kernel(own, peer, ready, chip):
    lower = lax.axis_index("gz") % 2 == 0
    mine, theirs = parts_of(own), parts_of(peer)
    put(chip, join(choose(lower, mine, theirs), choose(lower, theirs, mine)))


def ring_kernel(position, m0, m1, m2, m3, plane, buf):
    mine = position(lax.axis_index("gz"))
    for k, got in zip(distances(lax.axis_index("gz")), (m0, m1, m2, m3)):
        buf[mine ^ k] = got[...]
    s = [parts_of(buf.at[j]) for j in range(4)]
    put(plane, join(join(s[0], s[1]), join(s[2], s[3])))


def descend(mine, s, ql, qr):
    lower, upper = join(s[0], s[1]), join(s[2], s[3])
    q = middle(lower, upper, ql, qr)
    up = mine // 2 == 1
    ql, qr = jnp.where(up, -q, ql), jnp.where(up, qr, q)
    q = middle(choose(up, s[2], s[0]), choose(up, s[3], s[1]), ql, qr)
    up = mine % 2 == 1
    return jnp.where(up, -q, ql), jnp.where(up, qr, q)


def finish_kernel(
    own, peer, c0, c1, c2, c3, p0, p1, p2, p3, local, gpz, gsz, out, cbuf, pbuf
):
    iy, ix = position_y(lax.axis_index("gz")), position_x(lax.axis_index("gz"))
    for k, (c, p) in zip(distances(lax.axis_index("gz")), ((c0, p0), (c1, p1), (c2, p2), (c3, p3))):
        cbuf[iy ^ k] = c[...]
        pbuf[ix ^ k] = p[...]
    column = [parts_of(cbuf.at[j]) for j in range(4)]
    whole = [parts_of(pbuf.at[j]) for j in range(4)]
    a, d, b, e, f = join(join(whole[0], whole[1]), join(whole[2], whole[3]))
    inv = 1.0 / (b * f - e * e)
    ql, qr = (e * d - f * a) * inv, (e * a - b * d) * inv
    ql, qr = descend(ix, whole, ql, qr)
    ql, qr = descend(iy, column, ql, qr)
    lower = lax.axis_index("gz") % 2 == 0
    mine, theirs = parts_of(own), parts_of(peer)
    q = middle(choose(lower, mine, theirs), choose(lower, theirs, mine), ql, qr)
    ql, qr = jnp.where(lower, ql, -q), jnp.where(lower, q, qr)
    planes = ql.shape[0]
    depth = out.shape[0] // planes
    for p in range(planes):
        i = p * depth
        out[i : i + depth, :] = (
            local[i : i + depth, :]
            + gsz[i : i + depth, :] * ql[p : p + 1, :]
            + gpz[i : i + depth, :] * qr[p : p + 1, :]
        )


def distances(z):
    core = z % 2
    return 0, 1, 3 - core, 2 + core


def chain_of(value, count, unit):
    far = lax.ppermute(value, "gz", [(i, i ^ ((3 - i % 2) * unit)) for i in range(count)])
    near = lax.ppermute(value, "gz", [(i, i ^ unit) for i in range(count)])
    rest = lax.ppermute(far, "gz", [(i, i ^ 1) for i in range(count)])
    return [value, near, far, rest]


def position_y(z):
    return z // 2 % 4


def position_x(z):
    return z // 8


def partners(value, axis, count, unit):
    got = {
        k: lax.ppermute(value, axis, [(i, i ^ (k * unit) ^ (unit > 1)) for i in range(count)])
        for k in (1, 2, 3)
    }
    got[2], got[3] = got[2] * unity(), got[3] * unity()
    got[2] = lax.optimization_barrier(got[2]) * unity()
    return [got[k] for k in (1, 2, 3)]


def unity():
    return jnp.where(lax.axis_index("gz") < lax.axis_size("gz"), 1.0, 0.0)


def chip_neighbours(rows, peers):
    pairs = []
    for y in range(rows):
        for z in range(peers):
            end = z in (0, peers - 1)
            to = ((y ^ 1) * peers + z) if end else (y * peers + (z + 1 if z % 2 else z - 1))
            pairs.append((y * peers + z, to))
    return pairs


def shards(fields, cond_x, cond_y, cond_z, coupling):
    nf, nx, nz, ny = fields.shape
    planes, lines = nf * nx, nf * nx * nz
    peers = lax.axis_size("gz")
    steps = ny // SUB
    tall, flat, face, ends = (steps, SUB, lines), (lines, ny), (planes, ny), (5, planes, ny)
    hbm = pl.BlockSpec(memory_space=pltpu.HBM)
    dma = pltpu.SemaphoreType.DMA
    u, ky, kz, low, high, inner, outer = call(
        load_kernel, [flat] * 3 + [(2, *face)] * 4, [dma((3,))], 100_000, [hbm] * 3,
        fields.reshape(flat), cond_y.reshape(flat), cond_z.reshape(flat), vmem=53,
    )
    inner = lax.ppermute(inner, "gz", [(i, i ^ 1) for i in range(peers)])
    outer = lax.ppermute(outer, ("gy", "gz"), chip_neighbours(lax.axis_size("gy"), peers))
    gpy, gsy, ymat, gpz, gsz, zmat, r0 = call(
        factor_kernel,
        [tall, tall, (8, lines), flat, flat, (3, *face), flat],
        [(ny, lines)] + [tall] * 5 + [(nz, *face)],
        4_000_000,
        [VMEM] * 5,
        cond_x, coupling[None], u, ky, kz,
    )
    base, gp_edge, gs_edge, gp_rows, gs_rows = call(
        y_base_kernel, [(8, lines)] + [(2 * planes, ny)] * 2 + [flat] * 2, [(ny, lines)], 1_000_000, [VMEM] * 4,
        r0, gpy, gsy, ymat,
    )
    outer = outer * unity()
    msg, change = call(
        functools.partial(y_ends_kernel, peers), [(8, lines), (2 * planes, ny)], [], 100_000,
        [VMEM] * 7,
        low, high, inner, outer, base, gp_edge, gs_edge,
    )
    others = partners(msg, "gy", 4, 1)
    rz0, zends = call(
        functools.partial(y_local_kernel, peers), [flat, (3, *face)], [(ny, lines), tall, tall],
        1_000_000, [VMEM] * 11,
        u, r0, change, low, high, inner, outer, zmat, gpy, gsy, ymat,
    )
    rz, own = call(
        y_finish_kernel, [flat, ends], [(4, 8, lines)], 1_000_000, [VMEM] * 10,
        msg, *others, rz0, gp_rows, gs_rows, gpz, gsz, zends,
    )
    peer = lax.ppermute(own, "gz", [(i, i ^ 1) for i in range(peers)])
    local, ready = call(z_local_kernel, [flat, (8, 128)], [], 1_000_000, [VMEM] * 5, u, rz, gpz, gsz, zmat)
    [chip] = call(core_kernel, [ends], [], 50_000, [VMEM] * 3, own, peer, ready)
    column = chain_of(chip, peers, 2)
    [plane] = call(
        functools.partial(ring_kernel, position_y), [ends], [(4, *ends)], 50_000,
        [VMEM] * 4, *column,
    )
    whole = chain_of(plane, peers, 8)
    [out] = call(
        finish_kernel, [flat], [(4, *ends), (4, *ends)], 1_000_000, [VMEM] * 13,
        own, peer, *column, *whole, local, gpz, gsz,
    )
    return out.reshape(fields.shape)


def solution(mesh):
    block = P(None, None, "gz", "gy")
    return jax.shard_map(
        shards,
        mesh=mesh,
        in_specs=(block, P(), block, block, P()),
        out_specs=block,
        check_vma=False,
    )
```

```python
import functools

import jax
import jax.numpy as jnp
from jax import lax
from jax.experimental import pallas as pl
from jax.experimental.pallas import tpu as pltpu
from jax.sharding import PartitionSpec as P

SUB = 8
F32 = jnp.float32
VMEM = pl.BlockSpec(memory_space=pltpu.VMEM)
SMEM = pl.BlockSpec(memory_space=pltpu.SMEM)


def strided(ref, start, count, stride):
    return ref[pl.ds(start, count, stride=stride), :]


def load_kernel(uh, kyh, kzh, u, ky, kz, low, high, inner, outer, sem):
    copies = [
        pltpu.make_async_copy(src, dst, sem.at[i])
        for i, (src, dst) in enumerate(((uh, u), (kzh, kz), (kyh, ky)))
    ]
    for copy in copies:
        copy.start()
    planes = low.shape[1]
    depth = u.shape[0] // planes
    even = lax.axis_index("gz") % 2 == 0
    for i, array in enumerate((u, kz)):
        copies[i].wait()
        for p in range(planes):
            at = p * depth
            bottom, top = array[at : at + 1, :], array[at + depth - 1 : at + depth, :]
            low[i, p : p + 1, :] = bottom
            high[i, p : p + 1, :] = top
            inner[i, p : p + 1, :] = jnp.where(even, top, bottom)
            outer[i, p : p + 1, :] = jnp.where(even, bottom, top)
    copies[2].wait()


def factor_kernel(
    cx, cp, u, ky, kz, gpy, gsy, ymat, gpz, gsz, zmat, r0, kt, zr, wa, wb, wc, wd, zz
):
    lines, length = ky.shape
    steps = length // SUB
    planes, depth = zmat.shape[1], lines // zmat.shape[1]
    kt[...] = ky[...].T
    first = strided(kt, 0, SUB, steps)
    here = first
    for t in range(steps):
        after = strided(kt, t + 1, SUB, steps) if t + 1 < steps else pltpu.roll(first, SUB - 1, 0)
        zr[t] = 4.0 / (here + after)
        here = after
    last = strided(kt, steps - 1, SUB, steps)
    row = lax.broadcasted_iota(jnp.int32, (SUB, lines), 0)
    one, zero = jnp.ones((SUB, lines), F32), jnp.zeros((SUB, lines), F32)
    aw, aj, bw, bj = one, zero, zero, one
    for t in range(steps):
        wa[t], wb[t] = aw, bw
        aj, bj = aj + aw, bj + bw
        aw, bw = aw + zr[t] * aj, bw + zr[t] * bj
    cw, cj, dw, dj = one, zero, zero, one
    for t in reversed(range(steps)):
        wc[t], wd[t] = cw, dw
        cj, dj = cj + cw, dj + dw
        z = zr[t - 1] if t else pltpu.roll(zr[steps - 1], 1, 0)
        cw, dw = cw + z * cj, dw + z * dj
    al, be, ga, de = one, zero, one, zero
    for j in range(SUB - 1):
        nal, nbe = pltpu.roll(aw * al + bw * be, 1, 0), pltpu.roll(aj * al + bj * be, 1, 0)
        al, be = jnp.where(row == j + 1, nal, al), jnp.where(row == j + 1, nbe, be)
        nga = pltpu.roll(cw * ga + dw * de, SUB - 1, 0)
        nde = pltpu.roll(cj * ga + dj * de, SUB - 1, 0)
        at = SUB - 2 - j
        ga, de = jnp.where(row == at, nga, ga), jnp.where(row == at, nde, de)
    iw = 1.0 / (aj * al + bj * be)[SUB - 1 :, :]
    iv = 1.0 / (cj * ga + dj * de)[:1, :]
    al, be, ga, de = al * iw, be * iw, ga * iv, de * iv
    for t in range(steps):
        gpy[t] = al * wa[t] + be * wb[t]
        gsy[t] = ga * wc[t] + de * wd[t]
    ymat[...] = jnp.zeros_like(ymat)
    ymat[2:3, :] = gsy[0][:1, :]
    ymat[3:4, :] = iw
    ymat[4:5, :] = gpy[steps - 1][SUB - 1 :, :]
    ymat[5:6, :] = first[:1, :]
    ymat[6:7, :] = last[SUB - 1 :, :]
    here = [kz[pl.ds(p * depth, 1), :] for p in range(planes)]
    here = jnp.concatenate(here, 0)
    for t in range(depth - 1):
        after = jnp.concatenate([kz[pl.ds(p * depth + t + 1, 1), :] for p in range(planes)], 0)
        zz[t] = 4.0 / (here + after)
        here = after
    w, j = jnp.ones_like(here), jnp.zeros_like(here)
    ws = []
    for t in range(depth):
        ws.append(w)
        j = j + w
        if t + 1 < depth:
            w = w + zz[t] * j
    ij = 1.0 / j
    for t in range(depth):
        g = ws[t] * ij
        for p in range(planes):
            gpz[pl.ds(p * depth + t, 1), :] = g[p : p + 1, :]
    zmat[1] = ij
    zmat[2] = ws[depth - 1] * ij
    w, j = jnp.ones_like(here), jnp.zeros_like(here)
    ws = []
    for t in reversed(range(depth)):
        ws.append(w)
        j = j + w
        if t:
            w = w + zz[t - 1] * j
    ij = 1.0 / j
    for t in range(depth):
        g = ws[depth - 1 - t] * ij
        for p in range(planes):
            gsz[pl.ds(p * depth + t, 1), :] = g[p : p + 1, :]
    zmat[0] = ws[depth - 1] * ij
    for f in range(2):
        for x in range(2):
            at = (f * 2 + x) * depth
            me = u[at : at + depth, :]
            beside = u[(f * 2 + 1 - x) * depth : (f * 2 + 2 - x) * depth, :]
            other = u[((1 - f) * 2 + x) * depth : ((1 - f) * 2 + x + 1) * depth, :]
            face = 0.5 * (cx[f : f + 1, 0:1] + cx[f : f + 1, 1:2])
            k = kz[at : at + depth, :]
            flux = 0.5 * (k[1:] + k[:-1]) * (me[1:] - me[:-1])
            none = jnp.zeros((1, length), F32)
            flow = jnp.concatenate([flux, none], 0) - jnp.concatenate([none, flux], 0)
            r0[at : at + depth, :] = (
                (2.0 - 0.5 * cx[f : f + 1, x : x + 1]) * me
                + face * (beside - me)
                + cp[:, x : x + 1] * (other - me)
                + flow
            )


def y_base_kernel(r0, gpy, gsy, ymat, base, gp_edge, gs_edge, gp_rows, gs_rows, rt):
    steps, _, lines = gpy.shape
    planes = gp_edge.shape[0] // 2
    depth = lines // planes
    rt[...] = r0[...].T
    s = jnp.zeros((SUB, lines), F32)
    q = jnp.zeros((SUB, lines), F32)
    for t in range(steps):
        r = strided(rt, t, SUB, steps)
        s, q = s + gpy[t] * r, q + gsy[t] * r
    base[...] = ymat[...]
    base[0:1, :] = jnp.sum(q, axis=0, keepdims=True)
    base[1:2, :] = jnp.sum(s, axis=0, keepdims=True)
    for g, edge, rows in ((gpy, gp_edge, gp_rows), (gsy, gs_edge, gs_rows)):
        for t in range(steps):
            rt[pl.ds(t, SUB, stride=steps), :] = g[t]
        rows[...] = rt[...].T
        for p in range(planes):
            edge[p : p + 1, :] = rows[p * depth : p * depth + 1]
            edge[planes + p : planes + p + 1, :] = rows[(p + 1) * depth - 1 : (p + 1) * depth]


def y_ends_kernel(peers, low, high, inner, outer, base, gp_edge, gs_edge, msg, change):
    planes, lines = low.shape[1], base.shape[1]
    depth = lines // planes
    under = jnp.where(lax.axis_index("gz") > 0, 1.0, 0.0)
    over = jnp.where(lax.axis_index("gz") < peers - 1, 1.0, 0.0)
    even = lax.axis_index("gz") % 2 == 0
    below = [jnp.where(even, outer[i], inner[i]) * under for i in range(2)]
    above = [jnp.where(even, inner[i], outer[i]) * over for i in range(2)]
    lo = 0.5 * (below[1] + low[1]) * (below[0] - low[0])
    hi = 0.5 * (above[1] + high[1]) * (above[0] - high[0])
    both = jnp.concatenate([lo, hi], 0)
    change[...] = both
    row = lax.broadcasted_iota(jnp.int32, (2 * planes, lines), 0)
    line = lax.broadcasted_iota(jnp.int32, (2 * planes, lines), 1)
    here = line == jnp.where(row < planes, row * depth, (row - planes + 1) * depth - 1)
    msg[...] = base[...]
    for i, edge in enumerate((gs_edge, gp_edge)):
        ends = jnp.sum(edge[...] * both, axis=1, keepdims=True)
        added = jnp.sum(jnp.where(here, ends, 0.0), axis=0, keepdims=True)
        msg[i : i + 1, :] = base[i : i + 1, :] + added


def y_local_kernel(
    peers, u, r0, change, low, high, inner, outer, zmat, gpy, gsy, ymat, rz0, zends, rt, ss, qq
):
    steps, _, lines = gpy.shape
    planes, length = low.shape[1:]
    depth = lines // planes
    row = lax.broadcasted_iota(jnp.int32, (SUB, length), 0)
    parts = []
    for p in range(planes):
        i = p * depth
        top, mid, end = r0[i : i + SUB], r0[i + SUB : i + depth - SUB], r0[i + depth - SUB : i + depth]
        parts += [
            jnp.where(row == 0, top + change[p : p + 1, :], top),
            mid,
            jnp.where(row == SUB - 1, end + change[planes + p : planes + p + 1, :], end),
        ]
    rt[...] = jnp.concatenate(parts, 0).T
    s = jnp.zeros((SUB, lines), F32)
    q = jnp.zeros((SUB, lines), F32)
    for t in range(steps):
        back = steps - 1 - t
        s = s + gpy[t] * strided(rt, t, SUB, steps)
        ss[t] = s
        qq[back] = q
        q = q + gsy[back] * strided(rt, back, SUB, steps)
    row = lax.broadcasted_iota(jnp.int32, (SUB, lines), 0)
    so, qo = jnp.zeros_like(s), jnp.zeros_like(q)
    for j in range(1, SUB):
        so = so + jnp.where(row >= j, pltpu.roll(s, j, 0), 0.0)
        qo = qo + jnp.where(row < SUB - j, pltpu.roll(q, SUB - j, 0), 0.0)
    w = 1.0 / ymat[3:4, :]
    for t in range(steps):
        rt[pl.ds(t, SUB, stride=steps), :] = gsy[t] * w * (ss[t] + so) + gpy[t] * w * (qq[t] + qo)
    rz0[...] = rt[...].T - 2.0 * u[...]
    under = jnp.where(lax.axis_index("gz") > 0, 0.0, 1.0)
    over = jnp.where(lax.axis_index("gz") < peers - 1, 1.0, 0.0)
    zends[0] = zmat[0] + under * 4.0 / low[1]
    zends[1] = zmat[1]
    above = jnp.where(lax.axis_index("gz") % 2 == 0, inner[1], outer[1])
    zends[2] = zmat[2] + 4.0 / (above * over + high[1])


def y_finish_kernel(m0, m1, m2, m3, rz0, gp_rows, gs_rows, gpz, gsz, zends, rz, own, buf):
    lines = m0.shape[1]
    planes = own.shape[1]
    depth = lines // planes
    got = (m0, m1, m2, m3)
    mine = lax.axis_index("gy")
    for k in range(4):
        buf[mine ^ k] = got[k][...]
    seg = []
    for j in range(4):
        s = buf[j]
        seg.append([s[i : i + 1, :] for i in range(7)])
    zero = jnp.zeros((1, lines), F32)
    gap = [4.0 / (seg[j][6] + seg[j + 1][5]) for j in range(3)]
    e, r = zero, 4.0 / seg[0][5]
    el, rl = e, r
    for j in range(3):
        a, d, b, c, f = seg[j][:5]
        inv = 1.0 / (r + b)
        e, r = d + c * (e - a) * inv, f - c * c * inv + gap[j]
        el, rl = jnp.where(mine == j + 1, e, el), jnp.where(mine == j + 1, r, rl)
    e, r = zero, 4.0 / seg[3][6]
    er, rr = e, r
    for j in (3, 2, 1):
        a, d, b, c, f = seg[j][:5]
        inv = 1.0 / (r + f)
        e, r = a + c * (e - d) * inv, b - c * c * inv + gap[j - 1]
        er, rr = jnp.where(mine == j - 1, e, er), jnp.where(mine == j - 1, r, rr)
    a, d, b, c, f = [m0[i : i + 1, :] for i in range(5)]
    left, right = b + rl, f + rr
    inv = 1.0 / (left * right - c * c)
    ql = ((el - a) * right - c * (er - d)) * inv
    qr = ((er - d) * left - c * (el - a)) * inv
    flux = jnp.concatenate([ql, qr, jnp.zeros((6, lines), F32)], 0).T
    for p in range(planes):
        rows = slice(p * depth, (p + 1) * depth)
        r = rz0[rows, :] + gs_rows[rows, :] * flux[rows, 0:1] + gp_rows[rows, :] * flux[rows, 1:2]
        rz[rows, :] = r
        own[0, p : p + 1, :] = jnp.sum(gsz[rows, :] * r, axis=0, keepdims=True)
        own[1, p : p + 1, :] = jnp.sum(gpz[rows, :] * r, axis=0, keepdims=True)
    for i in range(3):
        own[i + 2] = zends[i]


def z_local_kernel(u, rz, gpz, gsz, zmat, out, ready):
    ready[...] = jnp.zeros_like(ready)
    _, planes, length = zmat.shape
    depth = rz.shape[0] // planes
    for p in range(planes):
        w = 1.0 / zmat[1, p : p + 1, :]
        s = jnp.zeros((1, length), F32)
        ss = []
        for t in range(depth):
            at = pl.ds(p * depth + t, 1)
            s = s + gpz[at, :] * rz[at, :]
            ss.append(s)
        q = jnp.zeros((1, length), F32)
        for t in reversed(range(depth)):
            at = pl.ds(p * depth + t, 1)
            out[at, :] = u[at, :] + w * (gsz[at, :] * ss[t] + gpz[at, :] * q)
            q = q + gsz[at, :] * rz[at, :]


def call(kernel, outs, scratch, cost, in_specs, *args, vmem=32, out_spec=VMEM):
    return pl.pallas_call(
        kernel,
        out_shape=[jax.ShapeDtypeStruct(s, F32) for s in outs],
        in_specs=in_specs,
        out_specs=[out_spec] * len(outs),
        scratch_shapes=[pltpu.VMEM(s, F32) if isinstance(s, tuple) else s for s in scratch],
        compiler_params=pltpu.CompilerParams(vmem_limit_bytes=int(vmem * 2**20)),
        cost_estimate=pl.CostEstimate(flops=cost, bytes_accessed=cost // 4, transcendentals=0),
    )(*args)


def join(s, t):
    a1, d1, b1, e1, f1 = s
    a2, d2, b2, e2, f2 = t
    inv = 1.0 / (f1 + b2)
    jump = (a2 - d1) * inv
    cross = e1 * inv
    return (
        a1 + e1 * jump,
        d2 - e2 * jump,
        b1 - e1 * cross,
        e2 * cross,
        f2 - e2 * e2 * inv,
    )


def middle(s, t, ql, qr):
    return (t[0] - s[1] + t[3] * qr - s[3] * ql) / (s[4] + t[2])


def parts_of(ref):
    return tuple(ref[i] for i in range(5))


def choose(flag, s, t):
    return tuple(jnp.where(flag, a, b) for a, b in zip(s, t))


def put(ref, value):
    for i in range(5):
        ref[i] = value[i]


def core_kernel(own, peer, ready, chip):
    lower = lax.axis_index("gz") % 2 == 0
    mine, theirs = parts_of(own), parts_of(peer)
    put(chip, join(choose(lower, mine, theirs), choose(lower, theirs, mine)))


def ring_kernel(position, m0, m1, m2, m3, plane, buf):
    mine = position(lax.axis_index("gz"))
    for k, got in zip(distances(lax.axis_index("gz")), (m0, m1, m2, m3)):
        buf[mine ^ k] = got[...]
    s = [parts_of(buf.at[j]) for j in range(4)]
    put(plane, join(join(s[0], s[1]), join(s[2], s[3])))


def descend(mine, s, ql, qr):
    lower, upper = join(s[0], s[1]), join(s[2], s[3])
    q = middle(lower, upper, ql, qr)
    up = mine // 2 == 1
    ql, qr = jnp.where(up, -q, ql), jnp.where(up, qr, q)
    q = middle(choose(up, s[2], s[0]), choose(up, s[3], s[1]), ql, qr)
    up = mine % 2 == 1
    return jnp.where(up, -q, ql), jnp.where(up, qr, q)


def finish_kernel(
    own, peer, c0, c1, c2, c3, p0, p1, p2, p3, local, gpz, gsz, out, cbuf, pbuf, stage, sem
):
    iy, ix = position_y(lax.axis_index("gz")), position_x(lax.axis_index("gz"))
    for k, (c, p) in zip(distances(lax.axis_index("gz")), ((c0, p0), (c1, p1), (c2, p2), (c3, p3))):
        cbuf[iy ^ k] = c[...]
        pbuf[ix ^ k] = p[...]
    column = [parts_of(cbuf.at[j]) for j in range(4)]
    whole = [parts_of(pbuf.at[j]) for j in range(4)]
    a, d, b, e, f = join(join(whole[0], whole[1]), join(whole[2], whole[3]))
    inv = 1.0 / (b * f - e * e)
    ql, qr = (e * d - f * a) * inv, (e * a - b * d) * inv
    ql, qr = descend(ix, whole, ql, qr)
    ql, qr = descend(iy, column, ql, qr)
    lower = lax.axis_index("gz") % 2 == 0
    mine, theirs = parts_of(own), parts_of(peer)
    q = middle(choose(lower, mine, theirs), choose(lower, theirs, mine), ql, qr)
    ql, qr = jnp.where(lower, ql, -q), jnp.where(lower, q, qr)
    planes = ql.shape[0]
    depth = out.shape[0] // planes
    copies = []
    for p in range(planes):
        rows = slice(p * depth, (p + 1) * depth)
        stage[rows, :] = (
            local[rows, :] + gsz[rows, :] * ql[p : p + 1, :] + gpz[rows, :] * qr[p : p + 1, :]
        )
        copies.append(pltpu.make_async_copy(stage.at[rows, :], out.at[rows, :], sem.at[p]))
        copies[-1].start()
    for copy in copies:
        copy.wait()


def distances(z):
    core = z % 2
    return 0, 1, 3 - core, 2 + core


def chain_of(value, count, unit):
    far = lax.ppermute(value, "gz", [(i, i ^ ((3 - i % 2) * unit)) for i in range(count)])
    near = lax.ppermute(value, "gz", [(i, i ^ unit) for i in range(count)])
    rest = lax.ppermute(far, "gz", [(i, i ^ 1) for i in range(count)])
    return [value, near, far, rest]


def position_y(z):
    return z // 2 % 4


def position_x(z):
    return z // 8


def partners(value, axis, count, unit):
    got = {
        k: lax.ppermute(value, axis, [(i, i ^ (k * unit) ^ (unit > 1)) for i in range(count)])
        for k in (1, 2, 3)
    }
    got[2], got[3] = got[2] * unity(), got[3] * unity()
    got[2] = lax.optimization_barrier(got[2]) * unity()
    return [got[k] for k in (1, 2, 3)]


def unity():
    return jnp.where(lax.axis_index("gz") < lax.axis_size("gz"), 1.0, 0.0)


def chip_neighbours(rows, peers):
    pairs = []
    for y in range(rows):
        for z in range(peers):
            end = z in (0, peers - 1)
            to = ((y ^ 1) * peers + z) if end else (y * peers + (z + 1 if z % 2 else z - 1))
            pairs.append((y * peers + z, to))
    return pairs


def shards(fields, cond_x, cond_y, cond_z, coupling):
    nf, nx, nz, ny = fields.shape
    planes, lines = nf * nx, nf * nx * nz
    peers = lax.axis_size("gz")
    steps = ny // SUB
    tall, flat, face, ends = (steps, SUB, lines), (lines, ny), (planes, ny), (5, planes, ny)
    hbm = pl.BlockSpec(memory_space=pltpu.HBM)
    dma = pltpu.SemaphoreType.DMA
    u, ky, kz, low, high, inner, outer = call(
        load_kernel, [flat] * 3 + [(2, *face)] * 4, [dma((3,))], 100_000, [hbm] * 3,
        fields.reshape(flat), cond_y.reshape(flat), cond_z.reshape(flat), vmem=53,
    )
    inner = lax.ppermute(inner, "gz", [(i, i ^ 1) for i in range(peers)])
    outer = lax.ppermute(outer, ("gy", "gz"), chip_neighbours(lax.axis_size("gy"), peers))
    gpy, gsy, ymat, gpz, gsz, zmat, r0 = call(
        factor_kernel,
        [tall, tall, (8, lines), flat, flat, (3, *face), flat],
        [(ny, lines)] + [tall] * 5 + [(nz, *face)],
        4_000_000,
        [VMEM] * 5,
        cond_x, coupling[None], u, ky, kz,
    )
    base, gp_edge, gs_edge, gp_rows, gs_rows = call(
        y_base_kernel, [(8, lines)] + [(2 * planes, ny)] * 2 + [flat] * 2, [(ny, lines)], 1_000_000, [VMEM] * 4,
        r0, gpy, gsy, ymat,
    )
    outer = outer * unity()
    msg, change = call(
        functools.partial(y_ends_kernel, peers), [(8, lines), (2 * planes, ny)], [], 100_000,
        [VMEM] * 7,
        low, high, inner, outer, base, gp_edge, gs_edge,
    )
    others = partners(msg, "gy", 4, 1)
    rz0, zends = call(
        functools.partial(y_local_kernel, peers), [flat, (3, *face)], [(ny, lines), tall, tall],
        1_000_000, [VMEM] * 11,
        u, r0, change, low, high, inner, outer, zmat, gpy, gsy, ymat,
    )
    rz, own = call(
        y_finish_kernel, [flat, ends], [(4, 8, lines)], 1_000_000, [VMEM] * 10,
        msg, *others, rz0, gp_rows, gs_rows, gpz, gsz, zends,
    )
    peer = lax.ppermute(own, "gz", [(i, i ^ 1) for i in range(peers)])
    local, ready = call(z_local_kernel, [flat, (8, 128)], [], 1_000_000, [VMEM] * 5, u, rz, gpz, gsz, zmat)
    [chip] = call(core_kernel, [ends], [], 50_000, [VMEM] * 3, own, peer, ready)
    column = chain_of(chip, peers, 2)
    [plane] = call(
        functools.partial(ring_kernel, position_y), [ends], [(4, *ends)], 50_000,
        [VMEM] * 4, *column,
    )
    whole = chain_of(plane, peers, 8)
    [out] = call(
        finish_kernel, [flat], [(4, *ends), (4, *ends), flat, dma((planes,))], 1_000_000, [VMEM] * 13,
        own, peer, *column, *whole, local, gpz, gsz, out_spec=hbm,
    )
    return out.reshape(fields.shape)


def solution(mesh):
    block = P(None, None, "gz", "gy")
    return jax.shard_map(
        shards,
        mesh=mesh,
        in_specs=(block, P(), block, block, P()),
        out_specs=block,
        check_vma=False,
    )
```
